256 devices in a mesh: dp: 32 (over z_hi, x, core), fsdp: 8 (over z_lo, y).
Axes of the slice: x: 4, y: 4, z: 8 (z_hi: 4, z_lo: 2; z = z_hi * 2 + z_lo), core: 2. Of those that a mesh axis runs over, the one named last changes fastest.
Arguments:
- hidden: bfloat16 [256, 2, 256, 8192], P(('dp', 'fsdp')), may hold values from -6 to 6
- frozen_weight: bfloat16 [8192, 1024], P('fsdp'), may hold values from -0.0625 to 0.0625
- adapter_down_weight: bfloat16 [8192, 128], P('fsdp'), may hold values from -0.0625 to 0.0625
- adapter_up_weight: bfloat16 [2, 64, 512], replicated, may hold values from -0.75 to 0.75
- readout: bfloat16 [256, 2, 256, 512], P(('dp', 'fsdp')), may hold values from -0.25 to 0.25
- chosen: int32 [256], P(('dp', 'fsdp')), may hold values from 0 to 1
- response_length: int32 [256, 2], P(('dp', 'fsdp')), may hold values from 64 to 256, as said below
Outputs:
- grad_down: float32 [8192, 128], P('fsdp')
- grad_up: float32 [2, 64, 512], replicated
The draws below stay inside these ranges and needn't reach their ends.
Inputs may be any that keep to these rules, and one draw needn't show every extreme that they name: `chosen`: 0 names the first sequence of the pair, 1 the second. A sequence's response is its last response_length positions.
All inputs are finite; a program needn't handle non-finite values.
Results may differ from the reference program's by a relative error of at most 0.006.
Values may be sent and summed in bfloat16 or wider, within the bound.
A program may use at most 128 MiB of HBM per device.

```python
import jax
import jax.numpy as jnp
from jax import lax

MODEL_DIMENSION = 8192
ADAPTER_RANK = 64
SEQ = 256
KEY_VALUE_WIDTH = 512
PAIRS = 256


def draw_response_length(key, part):
    key = jax.random.fold_in(key, 7)
    first, second, third = jax.random.split(key, 3)
    lengths = jax.random.randint(first, (PAIRS, 2), SEQ // 4, SEQ + 1)
    row_pick = jax.random.randint(second, (), 0, PAIRS)
    col_pick = jax.random.randint(third, (), 0, 2)
    lengths = lengths.at[row_pick, col_pick].set(SEQ)
    lengths = lengths.at[row_pick, 1 - col_pick].set(SEQ // 4)
    return lengths.astype(jnp.int32)


def touch_ends(drawn, stream_key, smallest, largest):
    shape = drawn.shape
    place = [jax.random.randint(jax.random.fold_in(stream_key, axis), (), 0, shape[axis]) for axis in range(len(shape))]
    drawn = drawn.at[tuple(place)].set(smallest)
    longest = shape.index(max(shape))
    place[longest] = (place[longest] + 1) % shape[longest]
    return drawn.at[tuple(place)].set(largest)


def block_scale(own_key, shape, cuts, least, high):
    level = 1.0
    for dim, parts in cuts:
        heights = jax.random.uniform(jax.random.fold_in(jax.random.fold_in(own_key, 6), dim), (parts,), jnp.float32, least / len(cuts), high / len(cuts))
        level = level * jnp.repeat(jnp.exp(heights), shape[dim] // parts).reshape((-1,) + (1,) * (len(shape) - 1 - dim))
    return level


def scatter_about(stream_key, shape, scale, limit, cuts=(), held_as=jnp.bfloat16):
    loudness = block_scale(stream_key, shape, cuts, -0.22, 0.18) if cuts else 1.0
    result = jax.random.normal(stream_key, shape, jnp.float32) * scale * loudness
    return jnp.minimum(jnp.maximum(result, -limit), limit).astype(held_as)


def setup_inputs(seed: int = 0) -> dict:
    key_of = jax.random.split(jax.random.key(seed), 8)
    hidden = scatter_about(key_of[0], (PAIRS, 2, SEQ, MODEL_DIMENSION), 1.0, 6.0, ((0, 256),))
    frozen_weight = scatter_about(key_of[1], (MODEL_DIMENSION, 2 * KEY_VALUE_WIDTH), MODEL_DIMENSION ** -0.5, 0.0625, ((0, 8),))
    adapter_down_weight = scatter_about(key_of[2], (MODEL_DIMENSION, 2 * ADAPTER_RANK), MODEL_DIMENSION ** -0.5, 0.0625, ((0, 8),))
    adapter_up_weight = scatter_about(key_of[3], (2, ADAPTER_RANK, KEY_VALUE_WIDTH), ADAPTER_RANK ** -0.5, 0.75)
    readout = scatter_about(key_of[4], (PAIRS, 2, SEQ, KEY_VALUE_WIDTH), KEY_VALUE_WIDTH ** -0.5, 0.25, ((0, 256),))
    chosen = touch_ends(jax.random.randint(key_of[5], (PAIRS,), 0, 2), jax.random.fold_in(key_of[5], 1), 0, 1).astype(jnp.int32)
    response_length = draw_response_length(jax.random.fold_in(key_of[7], 71), 0)
    return {"hidden": hidden, "frozen_weight": frozen_weight, "adapter_down_weight": adapter_down_weight, "adapter_up_weight": adapter_up_weight, "readout": readout, "chosen": chosen, "response_length": response_length}


adapter_scale = 0.5
preference_beta = 0.1


def reference(hidden, frozen_weight, adapter_down_weight, adapter_up_weight, readout, chosen, response_length):
    def one_pair(totals, pair_item):
        tokens, reads, picked, lengths = pair_item
        token_row_block = tokens.reshape(2 * SEQ, MODEL_DIMENSION)
        base_out = jnp.dot(token_row_block, frozen_weight, preferred_element_type=jnp.float32)
        projected_rows = jnp.dot(token_row_block, adapter_down_weight, preferred_element_type=jnp.float32).astype(jnp.bfloat16)
        reference_keys = base_out[:, :KEY_VALUE_WIDTH]
        reference_values = base_out[:, KEY_VALUE_WIDTH:]
        projected_keys = projected_rows[:, :ADAPTER_RANK]
        projected_values = projected_rows[:, ADAPTER_RANK:]
        policy_keys = reference_keys + adapter_scale * jnp.dot(projected_keys, adapter_up_weight[0], preferred_element_type=jnp.float32)
        policy_values = reference_values + adapter_scale * jnp.dot(projected_values, adapter_up_weight[1], preferred_element_type=jnp.float32)
        readout_rows = reads.reshape(2 * SEQ, KEY_VALUE_WIDTH).astype(jnp.float32)
        tok_ref = jnp.sum(readout_rows * reference_keys * reference_values, axis=1).reshape(2, SEQ)
        tok_pol = jnp.sum(readout_rows * policy_keys * policy_values, axis=1).reshape(2, SEQ)
        positions = jnp.arange(SEQ, dtype=jnp.int32)
        response_mask = (positions[None, :] >= (SEQ - lengths)[:, None]).astype(jnp.float32)
        seq_ref = jnp.sum(response_mask * tok_ref, axis=1)
        seq_pol = jnp.sum(response_mask * tok_pol, axis=1)
        pair_sign = jnp.where(jnp.arange(2, dtype=jnp.int32) == picked, jnp.float32(1.0), jnp.float32(-1.0))
        margin = jnp.sum(pair_sign * (seq_pol - seq_ref))
        pair_weight = -preference_beta * jax.nn.sigmoid(-preference_beta * margin)
        coeff = (pair_weight * pair_sign[:, None] * response_mask).reshape(2 * SEQ, 1)
        key_gradient = (coeff * readout_rows * policy_values).astype(jnp.bfloat16)
        value_gradient = (coeff * readout_rows * policy_keys).astype(jnp.bfloat16)
        up_term = jnp.stack([
            adapter_scale * jnp.dot(projected_keys.T, key_gradient, preferred_element_type=jnp.float32),
            adapter_scale * jnp.dot(projected_values.T, value_gradient, preferred_element_type=jnp.float32)])
        back = jnp.concatenate([
            adapter_scale * jnp.dot(key_gradient, adapter_up_weight[0].T, preferred_element_type=jnp.float32),
            adapter_scale * jnp.dot(value_gradient, adapter_up_weight[1].T, preferred_element_type=jnp.float32)], axis=1).astype(jnp.bfloat16)
        down_term = jnp.dot(token_row_block.T, back, preferred_element_type=jnp.float32)
        return (totals[0] + down_term, totals[1] + up_term), None

    start = (jnp.zeros((MODEL_DIMENSION, 2 * ADAPTER_RANK), jnp.float32), jnp.zeros((2, ADAPTER_RANK, KEY_VALUE_WIDTH), jnp.float32))
    totals, unused = lax.scan(one_pair, start, (hidden, readout, chosen, response_length))
    return totals[0], totals[1]
```

```python
import jax
import jax.numpy as jnp
from jax import lax
from jax.experimental import pallas as pl
from jax.experimental.pallas import tpu as pltpu
from jax.sharding import PartitionSpec as P

MESH = pl.DeviceIdType.MESH
F32 = jnp.float32
BF16 = jnp.bfloat16
adapter_scale = 0.5
preference_beta = 0.1

HALF = 512
COMMON = 96
SHARE = 80
WIDE = 1152


def kernel(
    hid, fw, ad, up_h, ro_h, chosen, lengths, od, ou,
    W, H, acc, R, up, ro, pol, low, gk, gv, BT, U, UT, US1, US2, UA, UB,
    D, RZ, E, D2, RY, S1, S2, G, GT,
    loc, hs, hr, ys, yr, zs, zr, xs, xr, ps, pr, ts, tr, us, ur, vs, vr, qs, qr, ws, wr, ss, sr, gs, gr,
):
    dp = lax.axis_index("dp")
    fs = lax.axis_index("fsdp")
    zh, x, c = dp // 8, (dp // 2) % 4, dp % 2
    zl, y = fs // 4, fs % 4
    me16 = dp // 2
    z = zh * 2 + zl

    def dev(zh_, x_, c_, zl_, y_):
        return ((zh_ * 4 + x_) * 2 + c_, zl_ * 4 + y_)

    def at_y(n):
        return dev(zh, x, c, zl, (y + n + 4) % 4)

    def at_z(n):
        zz = (z + n + 8) % 8
        return dev(zz // 2, x, c, zz % 2, y)

    twin = dev(zh, x, 1 - c, zl, y)
    pa, pb = x % 2, x // 2
    x_a = dev(zh, x + 1 - 2 * pa, c, zl, y)
    x_b = dev(zh, (x + 3 + 2 * pa) % 4, c, zl, y)
    y_to = (at_y(1), at_y(-1))
    z_to = (at_z(1), at_z(-1))
    x_to = (x_a, x_b)

    def peer16(k):
        j = (me16 + k) % 16
        return (j * 2 + c, fs)

    def peer8(k):
        return (dp, (fs + k) % 8)

    def rc(src, dst, s, r, d):
        return pltpu.make_async_remote_copy(
            src_ref=src, dst_ref=dst, send_sem=s, recv_sem=r, device_id=d, device_id_type=MESH
        )

    mine = fs
    w_in = [
        pltpu.make_async_copy(
            fw.at[pl.ds(pl.multiple_of(c * HALF, HALF), HALF), :],
            W.at[mine, :, pl.ds(0, 1024)], loc.at[0]),
        pltpu.make_async_copy(
            ad.at[pl.ds(pl.multiple_of(c * HALF, HALF), HALF), :],
            W.at[mine, :, pl.ds(1024, 128)], loc.at[1]),
    ]
    others_in = [
        pltpu.make_async_copy(ro_h.at[0], ro, loc.at[2]),
        pltpu.make_async_copy(up_h, up, loc.at[3]),
    ]

    def h_cols(p, core):
        return pl.ds(pl.multiple_of(p * 1024 + core * HALF, HALF), HALF)

    h_in = [
        pltpu.make_async_copy(hid.at[0, :, :, h_cols(p, c)], H.at[p, pl.ds(0, 2)], loc.at[4 + p])
        for p in range(8)
    ]
    for cp in w_in + h_in + others_in:
        cp.start()

    bar = pltpu.get_barrier_semaphore()
    z_other = at_z(2 * zl - 1)
    pl.semaphore_signal(bar, inc=1, device_id=twin, device_id_type=MESH)
    pl.semaphore_signal(bar, inc=1, device_id=z_other, device_id_type=MESH)
    for k in range(1, 8):
        pl.semaphore_signal(bar, inc=1, device_id=peer8(k), device_id_type=MESH)
    for k in range(1, 16):
        pl.semaphore_signal(bar, inc=1, device_id=peer16(k), device_id_type=MESH)
    pl.semaphore_wait(bar, 24)

    started = []

    def go(cp):
        cp.start()
        started.append(cp)

    h_out = [
        rc(hid.at[0, :, :, h_cols(p, 1 - c)], H.at[p, pl.ds(2, 2)], hs.at[p], hr.at[p], twin)
        for p in range(8)
    ]

    def piece(dz, dy):
        zz = zl if dz == 0 else 1 - zl
        return zz * 4 + (y + dy) % 4

    def rows_share(d, other=False):
        par = pa if d == 0 else pb
        if other:
            par = 1 - par
        base = 2 * COMMON + d * 2 * SHARE
        return pl.ds(pl.multiple_of(base + SHARE * par, 16), SHARE)

    def rows_common(d):
        return pl.ds(COMMON * d, COMMON)

    def y_msg(d, m, received):
        step = 1 - 2 * d
        back = 1 if m in (2, 4) else 0
        dy = -step * (back + (1 if received else 0))
        rows = {0: rows_share(d), 1: rows_common(d), 2: rows_share(d), 3: rows_share(1 - d),
                4: rows_common(d), 5: rows_common(1 - d)}[m]
        ref = W.at[piece(0, dy % 4), rows, :]
        return rc(ref, ref, ys.at[d, m], yr.at[d, m], y_to[d])

    def z_msg(d, dy, m, received):
        rows = rows_share(d) if m == 0 else rows_common(d)
        ref = W.at[piece(1 if received else 0, dy % 4), rows, :]
        return rc(ref, ref, zs.at[d, dy % 4, m], zr.at[d, dy % 4, m], z_to[d])

    def x_msg(d, dz, dy, received):
        ref = W.at[piece(dz, dy % 4), rows_share(d, received), :]
        i = dz * 4 + dy % 4
        return rc(ref, ref, xs.at[d, i], xr.at[d, i], x_to[d])

    def mm(p, first, blocks):
        @pl.loop(blocks[0], blocks[1])
        def _(tb):
            h = H[p, tb]
            for nb in range(3):
                cols = pl.ds(nb * 384, 384)
                r = jnp.dot(h, W[p, :, cols], preferred_element_type=F32)
                if first:
                    acc[tb, :, cols] = r
                else:
                    acc[tb, :, cols] += r

    for cp in w_in:
        cp.wait()
    for d in range(2):
        go(y_msg(d, 0, False))
        go(z_msg(d, 0, 0, False))
    for p in range(4):
        go(h_out[p])
    for d in range(2):
        go(y_msg(d, 1, False))
        go(z_msg(d, 0, 1, False))
    for p in range(4, 8):
        go(h_out[p])

    for d in range(2):
        s = 1 - 2 * d
        y_msg(d, 0, True).wait_recv()
        go(y_msg(d, 2, False))
        go(y_msg(d, 3, False))
        go(z_msg(d, -s, 0, False))
        go(x_msg(d, 0, -s, False))
    for d in range(2):
        z_msg(d, 0, 0, True).wait_recv()
        go(x_msg(d, 1, 0, False))
    for d in range(2):
        s = 1 - 2 * d
        y_msg(d, 1, True).wait_recv()
        go(y_msg(d, 4, False))
        go(y_msg(d, 5, False))
        go(z_msg(d, -s, 1, False))
    for cp in h_in:
        cp.wait()
    for cp in h_out:
        cp.wait_recv()
    mm(piece(0, 0), True, (0, 4))
    for d in range(2):
        s = 1 - 2 * d
        y_msg(d, 2, True).wait_recv()
        go(z_msg(d, 2, 0, False))
        go(x_msg(d, 0, 2, False))
        z_msg(d, -s, 0, True).wait_recv()
        go(x_msg(d, 1, -s, False))
    for d in range(2):
        z_msg(d, 0, 1, True).wait_recv()
        x_msg(d, 1, 0, True).wait_recv()
    mm(piece(1, 0), False, (0, 4))
    for d in range(2):
        s = 1 - 2 * d
        y_msg(1 - d, 3, True).wait_recv()
        go(z_msg(d, s, 0, False))
        go(x_msg(d, 0, s, False))
    for d in range(2):
        y_msg(d, 4, True).wait_recv()
        go(z_msg(d, 2, 1, False))
        z_msg(d, 2, 0, True).wait_recv()
        go(x_msg(d, 1, 2, False))
    for d in range(2):
        s = 1 - 2 * d
        y_msg(1 - d, 5, True).wait_recv()
        go(z_msg(d, s, 1, False))
        z_msg(d, s, 0, True).wait_recv()
        go(x_msg(d, 1, s, False))
    for dy in (2, 1, 3):
        for d in range(2):
            x_msg(d, 0, dy, True).wait_recv()
        mm(piece(0, dy), False, (0, 4))
    for d in range(2):
        z_msg(d, 2, 1, True).wait_recv()
        x_msg(d, 1, 2, True).wait_recv()
    mm(piece(1, 2), False, (0, 4))
    for dy in (1, 3):
        for d in range(2):
            z_msg(d, dy, 1, True).wait_recv()
            x_msg(d, 1, dy, True).wait_recv()
        mm(piece(1, dy), False, (2, 4))
    part = [rc(acc.at[2 + s], R.at[s], ps.at[s], pr.at[s], twin) for s in range(2)]
    for cp in part:
        go(cp)
    for dy in (1, 3):
        mm(piece(1, dy), False, (0, 2))
    for cp in others_in:
        cp.wait()
    for cp in part:
        cp.wait_recv()

    for s in range(2):
        t = (acc[s, :, pl.ds(1024, 128)] + R[s, :, pl.ds(1024, 128)]).astype(BF16)
        low[pl.ds(s * 256, 256), :] = t
        for i in range(2):
            pol[s, :, pl.ds(i * 512, 512)] = adapter_scale * jnp.dot(
                t[:, i * 64:(i + 1) * 64], up[i], preferred_element_type=F32)

    def token_weight(s, r):
        pos = r * 32 + lax.broadcasted_iota(jnp.int32, (32, 1), 0)
        sign = jnp.where(chosen[0] == s, 1.0, -1.0).astype(F32)
        return jnp.where(pos >= 256 - lengths[0, s], sign, 0.0)

    total = jnp.zeros((32, 512), F32)
    for s in range(2):
        def first_pass(r, total, s=s):
            rows = pl.ds(pl.multiple_of(r * 32, 32), 32)
            kr = acc[s, rows, pl.ds(0, 512)] + R[s, rows, pl.ds(0, 512)]
            vr = acc[s, rows, pl.ds(512, 512)] + R[s, rows, pl.ds(512, 512)]
            kp = kr + pol[s, rows, pl.ds(0, 512)]
            vp = vr + pol[s, rows, pl.ds(512, 512)]
            pol[s, rows, pl.ds(0, 512)] = kp
            pol[s, rows, pl.ds(512, 512)] = vp
            read = ro[s, rows, :].astype(F32)
            return total + token_weight(s, r) * (read * (kp * vp - kr * vr))
        total = lax.fori_loop(0, 8, first_pass, total)
    margin = jnp.sum(jnp.sum(total, axis=0, keepdims=True), axis=1, keepdims=True)
    pair_weight = -preference_beta * jax.nn.sigmoid(-preference_beta * margin)

    for s in range(2):
        def second_pass(r, carry, s=s):
            rows = pl.ds(pl.multiple_of(r * 32, 32), 32)
            whole = pl.ds(pl.multiple_of(s * 256 + r * 32, 32), 32)
            read = (pair_weight * token_weight(s, r)) * ro[s, rows, :].astype(F32)
            gk[whole, :] = (read * pol[s, rows, pl.ds(512, 512)]).astype(BF16)
            gv[whole, :] = (read * pol[s, rows, pl.ds(0, 512)]).astype(BF16)
            return carry
        lax.fori_loop(0, 8, second_pass, 0)

    nt = (((1,), (1,)), ((), ()))
    for i, g in enumerate((gk, gv)):
        BT[0, pl.ds(i * 64, 64), :] = (adapter_scale * lax.dot_general(
            up[i], g[...], nt, preferred_element_type=F32)).astype(BF16)
    b_cp = rc(BT.at[0], BT.at[1], ts.at[0], tr.at[0], twin)
    go(b_cp)
    low_t = jnp.transpose(low[...].astype(F32)).astype(BF16)
    for i, g in enumerate((gk, gv)):
        U[i] = adapter_scale * jnp.dot(
            low_t[i * 64:(i + 1) * 64, :], g[...], preferred_element_type=F32)
    u_cp = rc(U.at[1 - c], UT, ts.at[1], tr.at[1], twin)
    go(u_cp)
    b_cp.wait_recv()

    def grad(p):
        own = jnp.dot(BT[0], H[p, pl.ds(0, 2)].reshape(512, 512), preferred_element_type=F32)
        return own + jnp.dot(BT[1], H[p, pl.ds(2, 2)].reshape(512, 512), preferred_element_type=F32)

    zd = []
    for dy in (2, 1, 3, 0):
        D[dy] = grad(piece(1, dy)).astype(BF16)
        for d in range(2):
            h = pl.ds(d * 64, 64)
            cp = rc(D.at[dy, h], RZ.at[dy, h], us.at[dy, d], ur.at[dy, d], z_to[d])
            go(cp)
            zd.append((dy, cp))

    u_cp.wait_recv()
    chip = U[c] + UT[...]
    for j in range(16):
        r, q = j // 4, j % 4
        US1[j] = chip[r * 16:(r + 1) * 16, q * 128:(q + 1) * 128].astype(BF16)

    def spread16(src, dst, send, recv):
        def one(k, carry):
            j = (me16 + k) % 16
            rc(src(j), dst.at[me16], send.at[k], recv.at[k], peer16(k)).start()
            return carry
        lax.fori_loop(1, 16, one, 0)

    def land16(src, dst, send, recv):
        def one(k, carry):
            j = (me16 + 16 - k) % 16
            rc(src(j), dst.at[j], send.at[k], recv.at[k], peer16(k)).wait_recv()
            return carry
        lax.fori_loop(1, 16, one, 0)

    def sent16(src, dst, send, recv):
        def one(k, carry):
            j = (me16 + k) % 16
            rc(src(j), dst.at[me16], send.at[k], recv.at[k], peer16(k)).wait_send()
            return carry
        lax.fori_loop(1, 16, one, 0)

    u_args = (lambda j: US1.at[j], US2, vs, vr)
    spread16(*u_args)
    US2[me16] = US1[me16]

    for dy in (2, 1, 3, 0):
        E[dy] = grad(piece(0, dy))
    yd = []
    for dy in (2, 1, 3, 0):
        for dd, cp in zd:
            if dd == dy:
                cp.wait_recv()
        t = E[dy] + RZ[dy].astype(F32)
        if dy:
            D2[dy] = t.astype(BF16)
            cp = rc(D2.at[dy], RY.at[dy], qs.at[dy], qr.at[dy], at_y(dy))
            go(cp)
            yd.append(cp)
        else:
            E[0] = t

    land16(*u_args)
    UA[...] = jnp.sum(US2[...].astype(F32), axis=0).astype(BF16)
    UB[fs] = UA[...]
    for k in range(1, 8):
        go(rc(UA, UB.at[fs], ws.at[k], wr.at[k], peer8(k)))

    for cp in yd:
        cp.wait_recv()
    t = E[0] + RY[1].astype(F32) + RY[2].astype(F32) + RY[3].astype(F32)
    S1[...] = jnp.transpose(t).astype(BF16).reshape(16, 32, 128)
    s_args = (lambda j: S1.at[j], S2, ss, sr)
    spread16(*s_args)
    S2[me16] = S1[me16]
    for k in range(1, 8):
        rc(UA, UB.at[(fs + 8 - k) % 8], ws.at[k], wr.at[k], peer8(k)).wait_recv()
    G[me16, pl.ds(32, 16), :] = jnp.sum(UB[...].astype(F32), axis=0).astype(BF16)
    land16(*s_args)
    G[me16, pl.ds(0, 32), :] = jnp.sum(S2[...].astype(F32), axis=0).astype(BF16)
    g_args = (lambda j: G.at[me16], G, gs, gr)
    spread16(*g_args)

    def land_g(k, carry):
        j = (me16 + 16 - k) % 16
        rc(G.at[j], G.at[j], gs.at[k], gr.at[k], peer16(k)).wait_recv()
        return carry
    lax.fori_loop(1, 16, land_g, 0)
    t_cp = rc(G, GT, ts.at[2], tr.at[2], twin)
    go(t_cp)

    def place(src, core):
        for j in range(16):
            od[pl.ds(pl.multiple_of(core * 512 + j * 32, 32), 32), :] = src[j, pl.ds(0, 32), :].astype(F32)
            ou[core, pl.ds((j // 4) * 16, 16), pl.ds((j % 4) * 128, 128)] = src[j, pl.ds(32, 16), :].astype(F32)

    place(G, c)
    t_cp.wait_recv()
    place(GT, 1 - c)

    for cp in started:
        cp.wait_send()
    sent16(*u_args)
    sent16(*s_args)
    sent16(*g_args)


def local(hidden, frozen_weight, adapter_down_weight, adapter_up_weight, readout, chosen, response_length):
    dma = pltpu.SemaphoreType.DMA
    vmem = pltpu.VMEM
    anywhere = pl.BlockSpec(memory_space=pl.ANY)
    smem = pl.BlockSpec(memory_space=pltpu.SMEM)
    return pl.pallas_call(
        kernel,
        out_shape=(
            jax.ShapeDtypeStruct((1024, 128), F32),
            jax.ShapeDtypeStruct((2, 64, 512), F32),
        ),
        in_specs=[anywhere] * 5 + [smem] * 2,
        out_specs=(pl.BlockSpec(memory_space=pltpu.VMEM), pl.BlockSpec(memory_space=pltpu.VMEM)),
        scratch_shapes=[
            vmem((8, HALF, WIDE), BF16),
            vmem((8, 4, 256, HALF), BF16),
            vmem((4, 256, WIDE), F32),
            vmem((2, 256, WIDE), F32),
            vmem((2, 64, 512), BF16),
            vmem((2, 256, 512), BF16),
            vmem((2, 256, 1024), F32),
            vmem((512, 128), BF16),
            vmem((512, 512), BF16),
            vmem((512, 512), BF16),
            vmem((2, 128, 512), BF16),
            vmem((2, 64, 512), F32),
            vmem((64, 512), F32),
            vmem((16, 16, 128), BF16),
            vmem((16, 16, 128), BF16),
            vmem((16, 128), BF16),
            vmem((8, 16, 128), BF16),
            vmem((4, 128, 512), BF16),
            vmem((4, 128, 512), BF16),
            vmem((4, 128, 512), F32),
            vmem((4, 128, 512), BF16),
            vmem((4, 128, 512), BF16),
            vmem((16, 32, 128), BF16),
            vmem((16, 32, 128), BF16),
            vmem((16, 48, 128), BF16),
            vmem((16, 48, 128), BF16),
            dma((12,)),
            dma((8,)), dma((8,)),
            dma((2, 6)), dma((2, 6)),
            dma((2, 4, 2)), dma((2, 4, 2)),
            dma((2, 8)), dma((2, 8)),
            dma((2,)), dma((2,)),
            dma((3,)), dma((3,)),
            dma((4, 2)), dma((4, 2)),
            dma((16,)), dma((16,)),
            dma((4,)), dma((4,)),
            dma((8,)), dma((8,)),
            dma((16,)), dma((16,)),
            dma((16,)), dma((16,)),
        ],
        compiler_params=pltpu.CompilerParams(
            collective_id=0, has_side_effects=True, vmem_limit_bytes=56 * 2**20
        ),
        cost_estimate=pl.CostEstimate(flops=12 * 10**9, bytes_accessed=12 * 10**6, transcendentals=1),
    )(hidden, frozen_weight, adapter_down_weight, adapter_up_weight, readout, chosen, response_length)


def solution(mesh):
    placed = (
        P(("dp", "fsdp"), None, None, None),
        P("fsdp", None),
        P("fsdp", None),
        P(),
        P(("dp", "fsdp"), None, None, None),
        P(("dp", "fsdp")),
        P(("dp", "fsdp"), None),
    )
    return jax.shard_map(
        local, mesh=mesh, in_specs=placed, out_specs=(P("fsdp", None), P()), check_vma=False
    )
```

```python
import jax
import jax.numpy as jnp
from jax import lax
from jax.experimental import pallas as pl
from jax.experimental.pallas import tpu as pltpu
from jax.sharding import PartitionSpec as P

MESH = pl.DeviceIdType.MESH
F32 = jnp.float32
BF16 = jnp.bfloat16
adapter_scale = 0.5
preference_beta = 0.1

HALF = 512
COMMON = 96
SHARE = 80
WIDE = 1152


def kernel(
    hid, fw, ad, up_h, ro_h, chosen, lengths, GD, GU,
    W, H, acc, R, L, RL, up, ro, pol, low, gk, gv, BT, U, UT, US1, US2, UA, UB,
    D, RZ, E, D2, RY, S1, S2,
    loc, hs, hr, ys, yr, zs, zr, xs, xr, ps, pr, ts, tr, us, ur, vs, vr, qs, qr, ws, wr, ss, sr, gs, gr, es, er,
):
    dp = lax.axis_index("dp")
    fs = lax.axis_index("fsdp")
    zh, x, c = dp // 8, (dp // 2) % 4, dp % 2
    zl, y = fs // 4, fs % 4
    me16 = dp // 2
    z = zh * 2 + zl

    def dev(zh_, x_, c_, zl_, y_):
        return ((zh_ * 4 + x_) * 2 + c_, zl_ * 4 + y_)

    def at_y(n):
        return dev(zh, x, c, zl, (y + n + 4) % 4)

    def at_z(n):
        zz = (z + n + 8) % 8
        return dev(zz // 2, x, c, zz % 2, y)

    twin = dev(zh, x, 1 - c, zl, y)
    pa, pb = x % 2, x // 2
    x_a = dev(zh, x + 1 - 2 * pa, c, zl, y)
    x_b = dev(zh, (x + 3 + 2 * pa) % 4, c, zl, y)
    y_to = (at_y(1), at_y(-1))
    z_to = (at_z(1), at_z(-1))
    x_to = (x_a, x_b)

    def peer16(k):
        j = (me16 + k) % 16
        return (j * 2 + c, fs)

    def peer8(k):
        return (dp, (fs + k) % 8)

    def rc(src, dst, s, r, d):
        return pltpu.make_async_remote_copy(
            src_ref=src, dst_ref=dst, send_sem=s, recv_sem=r, device_id=d, device_id_type=MESH
        )

    mine = fs
    w_in = [
        pltpu.make_async_copy(
            fw.at[pl.ds(pl.multiple_of(c * HALF, HALF), HALF), :],
            W.at[mine, :, pl.ds(0, 1024)], loc.at[0]),
        pltpu.make_async_copy(
            ad.at[pl.ds(pl.multiple_of(c * HALF, HALF), HALF), :],
            W.at[mine, :, pl.ds(1024, 128)], loc.at[1]),
    ]
    others_in = [
        pltpu.make_async_copy(ro_h.at[0], ro, loc.at[2]),
        pltpu.make_async_copy(up_h, up, loc.at[3]),
    ]

    def h_cols(p, core):
        return pl.ds(pl.multiple_of(p * 1024 + core * HALF, HALF), HALF)

    h_in = [
        pltpu.make_async_copy(hid.at[0, :, :, h_cols(p, c)], H.at[p, pl.ds(0, 2)], loc.at[4 + p])
        for p in range(8)
    ]
    for cp in w_in + h_in + others_in:
        cp.start()

    bar = pltpu.get_barrier_semaphore()
    z_other = at_z(2 * zl - 1)
    pl.semaphore_signal(bar, inc=1, device_id=twin, device_id_type=MESH)
    pl.semaphore_signal(bar, inc=1, device_id=z_other, device_id_type=MESH)
    for k in range(1, 8):
        pl.semaphore_signal(bar, inc=1, device_id=peer8(k), device_id_type=MESH)
    for k in range(1, 16):
        pl.semaphore_signal(bar, inc=1, device_id=peer16(k), device_id_type=MESH)
    pl.semaphore_wait(bar, 24)

    started = []

    def go(cp):
        cp.start()
        started.append(cp)

    h_out = [
        rc(hid.at[0, :, :, h_cols(p, 1 - c)], H.at[p, pl.ds(2, 2)], hs.at[p], hr.at[p], twin)
        for p in range(8)
    ]

    def piece(dz, dy):
        zz = zl if dz == 0 else 1 - zl
        return zz * 4 + (y + dy) % 4

    def rows_share(d, other=False):
        par = pa if d == 0 else pb
        if other:
            par = 1 - par
        base = 2 * COMMON + d * 2 * SHARE
        return pl.ds(pl.multiple_of(base + SHARE * par, 16), SHARE)

    def rows_common(d):
        return pl.ds(COMMON * d, COMMON)

    def y_msg(d, m, received):
        step = 1 - 2 * d
        back = 1 if m in (2, 4) else 0
        dy = -step * (back + (1 if received else 0))
        rows = {0: rows_share(d), 1: rows_common(d), 2: rows_share(d), 3: rows_share(1 - d),
                4: rows_common(d), 5: rows_common(1 - d)}[m]
        ref = W.at[piece(0, dy % 4), rows, :]
        return rc(ref, ref, ys.at[d, m], yr.at[d, m], y_to[d])

    def z_msg(d, dy, m, received):
        rows = rows_share(d) if m == 0 else rows_common(d)
        ref = W.at[piece(1 if received else 0, dy % 4), rows, :]
        return rc(ref, ref, zs.at[d, dy % 4, m], zr.at[d, dy % 4, m], z_to[d])

    def x_msg(d, dz, dy, received):
        ref = W.at[piece(dz, dy % 4), rows_share(d, received), :]
        i = dz * 4 + dy % 4
        return rc(ref, ref, xs.at[d, i], xr.at[d, i], x_to[d])

    def tokens(p, half):
        return H[p, pl.ds(half * 2, 2)].reshape(512, HALF)

    def mm(p, first, halves):
        for half in halves:
            for lo, n in ((0, 512), (512, 512), (1024, 128)):
                cols = pl.ds(lo, n)
                r = jnp.dot(tokens(p, half), W[p, :, cols], preferred_element_type=F32).reshape(2, 256, n)
                if first:
                    acc[pl.ds(half * 2, 2), :, cols] = r
                else:
                    acc[pl.ds(half * 2, 2), :, cols] += r

    def mm_last(half):
        p, q = piece(1, 1), piece(1, 3)

        @pl.loop(0, 3)
        def _(nb):
            cols = pl.ds(pl.multiple_of(nb * 384, 384), 384)
            r = jnp.dot(tokens(p, half), W[p, :, cols], preferred_element_type=F32)
            r += jnp.dot(tokens(q, half), W[q, :, cols], preferred_element_type=F32)
            r = r.reshape(2, 256, 384)
            if half:
                L[:, :, cols] = r.astype(BF16)
            else:
                acc[pl.ds(0, 2), :, cols] += r

    for cp in w_in:
        cp.wait()
    for d in range(2):
        go(y_msg(d, 0, False))
        go(z_msg(d, 0, 0, False))
    for p in range(4):
        go(h_out[p])
    for d in range(2):
        go(y_msg(d, 1, False))
        go(z_msg(d, 0, 1, False))
    for p in range(4, 8):
        go(h_out[p])

    for d in range(2):
        s = 1 - 2 * d
        y_msg(d, 0, True).wait_recv()
        go(y_msg(d, 2, False))
        go(y_msg(d, 3, False))
        go(z_msg(d, -s, 0, False))
        go(x_msg(d, 0, -s, False))
    for d in range(2):
        z_msg(d, 0, 0, True).wait_recv()
        go(x_msg(d, 1, 0, False))
    for d in range(2):
        s = 1 - 2 * d
        y_msg(d, 1, True).wait_recv()
        go(y_msg(d, 4, False))
        go(y_msg(d, 5, False))
        go(z_msg(d, -s, 1, False))
    for cp in h_in:
        cp.wait()
    for cp in h_out:
        cp.wait_recv()
    mm(piece(0, 0), True, (0, 1))
    for d in range(2):
        s = 1 - 2 * d
        y_msg(d, 2, True).wait_recv()
        go(z_msg(d, 2, 0, False))
        go(x_msg(d, 0, 2, False))
        z_msg(d, -s, 0, True).wait_recv()
        go(x_msg(d, 1, -s, False))
    for d in range(2):
        z_msg(d, 0, 1, True).wait_recv()
        x_msg(d, 1, 0, True).wait_recv()
    mm(piece(1, 0), False, (0, 1))
    for d in range(2):
        s = 1 - 2 * d
        y_msg(1 - d, 3, True).wait_recv()
        go(z_msg(d, s, 0, False))
        go(x_msg(d, 0, s, False))
    for d in range(2):
        y_msg(d, 4, True).wait_recv()
        go(z_msg(d, 2, 1, False))
        z_msg(d, 2, 0, True).wait_recv()
        go(x_msg(d, 1, 2, False))
    for d in range(2):
        s = 1 - 2 * d
        y_msg(1 - d, 5, True).wait_recv()
        go(z_msg(d, s, 1, False))
        z_msg(d, s, 0, True).wait_recv()
        go(x_msg(d, 1, s, False))
    for dy in (2, 1, 3):
        for d in range(2):
            x_msg(d, 0, dy, True).wait_recv()
        mm(piece(0, dy), False, (0, 1))
    for d in range(2):
        z_msg(d, 2, 1, True).wait_recv()
        x_msg(d, 1, 2, True).wait_recv()
    mm(piece(1, 2), False, (1,))
    early = rc(acc.at[pl.ds(2, 2)], R, ps.at[0], pr.at[0], twin)
    go(early)
    mm(piece(1, 2), False, (0,))
    for dy in (1, 3):
        for d in range(2):
            z_msg(d, dy, 1, True).wait_recv()
            x_msg(d, 1, dy, True).wait_recv()
    mm_last(1)
    late = rc(L, RL, ps.at[1], pr.at[1], twin)
    go(late)
    mm_last(0)
    for cp in others_in:
        cp.wait()
    early.wait_recv()
    late.wait_recv()

    for s in range(2):
        t = (acc[s, :, pl.ds(1024, 128)] + R[s, :, pl.ds(1024, 128)]
             + RL[s, :, pl.ds(1024, 128)].astype(F32)).astype(BF16)
        low[pl.ds(s * 256, 256), :] = t
        for i in range(2):
            pol[s, :, pl.ds(i * 512, 512)] = adapter_scale * jnp.dot(
                t[:, i * 64:(i + 1) * 64], up[i], preferred_element_type=F32)

    def token_weight(s, r):
        pos = r * 32 + lax.broadcasted_iota(jnp.int32, (32, 1), 0)
        sign = jnp.where(chosen[0] == s, 1.0, -1.0).astype(F32)
        return jnp.where(pos >= 256 - lengths[0, s], sign, 0.0)

    total = jnp.zeros((32, 512), F32)
    for s in range(2):
        def first_pass(r, total, s=s):
            rows = pl.ds(pl.multiple_of(r * 32, 32), 32)
            kr = acc[s, rows, pl.ds(0, 512)] + (
                R[s, rows, pl.ds(0, 512)] + RL[s, rows, pl.ds(0, 512)].astype(F32))
            vr = acc[s, rows, pl.ds(512, 512)] + (
                R[s, rows, pl.ds(512, 512)] + RL[s, rows, pl.ds(512, 512)].astype(F32))
            kp = kr + pol[s, rows, pl.ds(0, 512)]
            vp = vr + pol[s, rows, pl.ds(512, 512)]
            pol[s, rows, pl.ds(0, 512)] = kp
            pol[s, rows, pl.ds(512, 512)] = vp
            read = ro[s, rows, :].astype(F32)
            return total + token_weight(s, r) * (read * (kp * vp - kr * vr))
        total = lax.fori_loop(0, 8, first_pass, total)
    margin = jnp.sum(jnp.sum(total, axis=0, keepdims=True), axis=1, keepdims=True)
    pair_weight = -preference_beta * jax.nn.sigmoid(-preference_beta * margin)

    for s in range(2):
        def second_pass(r, carry, s=s):
            rows = pl.ds(pl.multiple_of(r * 32, 32), 32)
            whole = pl.ds(pl.multiple_of(s * 256 + r * 32, 32), 32)
            read = (pair_weight * token_weight(s, r)) * ro[s, rows, :].astype(F32)
            gk[whole, :] = (read * pol[s, rows, pl.ds(512, 512)]).astype(BF16)
            gv[whole, :] = (read * pol[s, rows, pl.ds(0, 512)]).astype(BF16)
            return carry
        lax.fori_loop(0, 8, second_pass, 0)

    nt = (((1,), (1,)), ((), ()))
    for i, g in enumerate((gk, gv)):
        BT[0, pl.ds(i * 64, 64), :] = (adapter_scale * lax.dot_general(
            up[i], g[...], nt, preferred_element_type=F32)).astype(BF16)
    b_cp = rc(BT.at[0], BT.at[1], ts.at[0], tr.at[0], twin)
    go(b_cp)
    low_t = jnp.transpose(low[...].astype(F32)).astype(BF16)
    for i, g in enumerate((gk, gv)):
        U[i] = adapter_scale * jnp.dot(
            low_t[i * 64:(i + 1) * 64, :], g[...], preferred_element_type=F32)
    u_cp = rc(U.at[1 - c], UT, ts.at[1], tr.at[1], twin)
    go(u_cp)
    b_cp.wait_recv()

    def grad(p):
        own = jnp.dot(BT[0], H[p, pl.ds(0, 2)].reshape(512, 512), preferred_element_type=F32)
        return own + jnp.dot(BT[1], H[p, pl.ds(2, 2)].reshape(512, 512), preferred_element_type=F32)

    zd = []
    for dy in (2, 1, 3, 0):
        D[dy] = grad(piece(1, dy)).astype(BF16)
        for d in range(2):
            h = pl.ds(d * 64, 64)
            cp = rc(D.at[dy, h], RZ.at[dy, h], us.at[dy, d], ur.at[dy, d], z_to[d])
            go(cp)
            zd.append((dy, cp))

    u_cp.wait_recv()
    chip = U[c] + UT[...]
    for j in range(16):
        r, q = j // 4, j % 4
        US1[j] = chip[r * 16:(r + 1) * 16, q * 128:(q + 1) * 128].astype(BF16)

    def spread16(src, dst, send, recv):
        def one(k, carry):
            j = (me16 + k) % 16
            rc(src(j), dst.at[me16], send.at[k], recv.at[k], peer16(k)).start()
            return carry
        lax.fori_loop(1, 16, one, 0)

    def land16(src, dst, send, recv):
        def one(k, carry):
            j = (me16 + 16 - k) % 16
            rc(src(j), dst.at[j], send.at[k], recv.at[k], peer16(k)).wait_recv()
            return carry
        lax.fori_loop(1, 16, one, 0)

    def sent16(src, dst, send, recv):
        def one(k, carry):
            j = (me16 + k) % 16
            rc(src(j), dst.at[me16], send.at[k], recv.at[k], peer16(k)).wait_send()
            return carry
        lax.fori_loop(1, 16, one, 0)

    u_args = (lambda j: US1.at[j], US2, vs, vr)
    spread16(*u_args)
    US2[me16] = US1[me16]

    for dy in (2, 1, 3, 0):
        E[dy] = grad(piece(0, dy))
    yd = []
    for dy in (2, 1, 3, 0):
        for dd, cp in zd:
            if dd == dy:
                cp.wait_recv()
        t = E[dy] + RZ[dy].astype(F32)
        if dy:
            D2[dy] = t.astype(BF16)
            cp = rc(D2.at[dy], RY.at[dy], qs.at[dy], qr.at[dy], at_y(dy))
            go(cp)
            yd.append(cp)
        else:
            E[0] = t

    land16(*u_args)
    UA[...] = jnp.sum(US2[...].astype(F32), axis=0).astype(BF16)
    UB[fs] = UA[...]
    for k in range(1, 8):
        go(rc(UA, UB.at[fs], ws.at[k], wr.at[k], peer8(k)))

    for cp in yd:
        cp.wait_recv()
    t = E[0] + RY[1].astype(F32) + RY[2].astype(F32) + RY[3].astype(F32)
    S1[...] = jnp.transpose(t).astype(BF16).reshape(16, 32, 128)
    s_args = (lambda j: S1.at[j], S2, ss, sr)
    spread16(*s_args)
    S2[me16] = S1[me16]
    for k in range(1, 8):
        rc(UA, UB.at[(fs + 8 - k) % 8], ws.at[k], wr.at[k], peer8(k)).wait_recv()
    GU[c, me16] = jnp.sum(UB[...].astype(F32), axis=0).astype(BF16)
    gu_args = (lambda j: GU.at[c, me16], GU.at[c], es, er)
    spread16(*gu_args)
    land16(*s_args)
    GD[c, me16] = jnp.sum(S2[...].astype(F32), axis=0).astype(BF16)
    gd_args = (lambda j: GD.at[c, me16], GD.at[c], gs, gr)
    spread16(*gd_args)
    land16(*gu_args)
    land16(*gd_args)
    out = [rc(GD.at[c], GD.at[c], ts.at[2], tr.at[2], twin), rc(GU.at[c], GU.at[c], ts.at[3], tr.at[3], twin)]
    for cp in out:
        go(cp)
    for cp in out:
        cp.wait_recv()
    for cp in started:
        cp.wait_send()
    for args in (u_args, s_args, gu_args, gd_args):
        sent16(*args)


def widen(gd, gu, od, ou):
    od[...] = gd[...].astype(F32).reshape(1024, 128)
    for core in range(2):
        for j in range(16):
            ou[core, pl.ds((j // 4) * 16, 16), pl.ds((j % 4) * 128, 128)] = gu[core, j].astype(F32)


def local(hidden, frozen_weight, adapter_down_weight, adapter_up_weight, readout, chosen, response_length):
    dma = pltpu.SemaphoreType.DMA
    vmem = pltpu.VMEM
    anywhere = pl.BlockSpec(memory_space=pl.ANY)
    smem = pl.BlockSpec(memory_space=pltpu.SMEM)
    gd, gu = pl.pallas_call(
        kernel,
        out_shape=(
            jax.ShapeDtypeStruct((2, 16, 32, 128), BF16),
            jax.ShapeDtypeStruct((2, 16, 16, 128), BF16),
        ),
        in_specs=[anywhere] * 5 + [smem] * 2,
        out_specs=(pl.BlockSpec(memory_space=pltpu.VMEM), pl.BlockSpec(memory_space=pltpu.VMEM)),
        scratch_shapes=[
            vmem((8, HALF, WIDE), BF16),
            vmem((8, 4, 256, HALF), BF16),
            vmem((4, 256, WIDE), F32),
            vmem((2, 256, WIDE), F32),
            vmem((2, 256, WIDE), BF16),
            vmem((2, 256, WIDE), BF16),
            vmem((2, 64, 512), BF16),
            vmem((2, 256, 512), BF16),
            vmem((2, 256, 1024), F32),
            vmem((512, 128), BF16),
            vmem((512, 512), BF16),
            vmem((512, 512), BF16),
            vmem((2, 128, 512), BF16),
            vmem((2, 64, 512), F32),
            vmem((64, 512), F32),
            vmem((16, 16, 128), BF16),
            vmem((16, 16, 128), BF16),
            vmem((16, 128), BF16),
            vmem((8, 16, 128), BF16),
            vmem((4, 128, 512), BF16),
            vmem((4, 128, 512), BF16),
            vmem((4, 128, 512), F32),
            vmem((4, 128, 512), BF16),
            vmem((4, 128, 512), BF16),
            vmem((16, 32, 128), BF16),
            vmem((16, 32, 128), BF16),
            dma((12,)),
            dma((8,)), dma((8,)),
            dma((2, 6)), dma((2, 6)),
            dma((2, 4, 2)), dma((2, 4, 2)),
            dma((2, 8)), dma((2, 8)),
            dma((2,)), dma((2,)),
            dma((4,)), dma((4,)),
            dma((4, 2)), dma((4, 2)),
            dma((16,)), dma((16,)),
            dma((4,)), dma((4,)),
            dma((8,)), dma((8,)),
            dma((16,)), dma((16,)),
            dma((16,)), dma((16,)),
            dma((16,)), dma((16,)),
        ],
        compiler_params=pltpu.CompilerParams(
            collective_id=0, has_side_effects=True, vmem_limit_bytes=56 * 2**20
        ),
        cost_estimate=pl.CostEstimate(flops=12 * 10**9, bytes_accessed=12 * 10**6, transcendentals=1),
    )(hidden, frozen_weight, adapter_down_weight, adapter_up_weight, readout, chosen, response_length)
    return pl.pallas_call(
        widen,
        out_shape=(
            jax.ShapeDtypeStruct((1024, 128), F32),
            jax.ShapeDtypeStruct((2, 64, 512), F32),
        ),
        in_specs=[pl.BlockSpec(memory_space=pltpu.VMEM)] * 2,
        out_specs=(pl.BlockSpec(memory_space=pltpu.VMEM),) * 2,
        cost_estimate=pl.CostEstimate(flops=10**6, bytes_accessed=2 * 10**6, transcendentals=0),
    )(gd, gu)


def solution(mesh):
    placed = (
        P(("dp", "fsdp"), None, None, None),
        P("fsdp", None),
        P("fsdp", None),
        P(),
        P(("dp", "fsdp"), None, None, None),
        P(("dp", "fsdp")),
        P(("dp", "fsdp"), None),
    )
    return jax.shard_map(
        local, mesh=mesh, in_specs=placed, out_specs=(P("fsdp", None), P()), check_vma=False
    )
```

```python
import jax
import jax.numpy as jnp
from jax import lax
from jax.experimental import pallas as pl
from jax.experimental.pallas import tpu as pltpu
from jax.sharding import PartitionSpec as P

MESH = pl.DeviceIdType.MESH
F32 = jnp.float32
BF16 = jnp.bfloat16
adapter_scale = 0.5
preference_beta = 0.1

HALF = 512
COMMON = 96
SHARE = 80
WIDE = 1152


def kernel(
    hid, fw, ad, up_h, ro_h, chosen, lengths, GD, GU,
    W, H, acc, R, L, RL, up, ro, pol, low, gk, gv, BT, U, UT, US1, US2, UA, UB,
    D, RZ, E, D2, RY, S1, S2,
    loc, hs, hr, ys, yr, zs, zr, xs, xr, ps, pr, ts, tr, us, ur, vs, vr, qs, qr, ws, wr, ss, sr, gs, gr, es, er, far,
):
    dp = lax.axis_index("dp")
    fs = lax.axis_index("fsdp")
    zh, x, c = dp // 8, (dp // 2) % 4, dp % 2
    zl, y = fs // 4, fs % 4
    me16 = dp // 2
    z = zh * 2 + zl

    def dev(zh_, x_, c_, zl_, y_):
        return ((zh_ * 4 + x_) * 2 + c_, zl_ * 4 + y_)

    def at_y(n):
        return dev(zh, x, c, zl, (y + n + 4) % 4)

    def at_z(n):
        zz = (z + n + 8) % 8
        return dev(zz // 2, x, c, zz % 2, y)

    twin = dev(zh, x, 1 - c, zl, y)
    pa, pb = x % 2, x // 2
    x_a = dev(zh, x + 1 - 2 * pa, c, zl, y)
    x_b = dev(zh, (x + 3 + 2 * pa) % 4, c, zl, y)
    y_to = (at_y(1), at_y(-1))
    z_to = (at_z(1), at_z(-1))
    x_to = (x_a, x_b)

    def peer16(k):
        j = (me16 + k) % 16
        return (j * 2 + c, fs)

    def peer8(k):
        return (dp, (fs + k) % 8)

    def rc(src, dst, s, r, d):
        return pltpu.make_async_remote_copy(
            src_ref=src, dst_ref=dst, send_sem=s, recv_sem=r, device_id=d, device_id_type=MESH
        )

    mine = fs
    w_in = [
        pltpu.make_async_copy(
            fw.at[pl.ds(pl.multiple_of(c * HALF, HALF), HALF), :],
            W.at[mine, :, pl.ds(0, 1024)], loc.at[0]),
        pltpu.make_async_copy(
            ad.at[pl.ds(pl.multiple_of(c * HALF, HALF), HALF), :],
            W.at[mine, :, pl.ds(1024, 128)], loc.at[1]),
    ]
    others_in = [
        pltpu.make_async_copy(ro_h.at[0], ro, loc.at[2]),
        pltpu.make_async_copy(up_h, up, loc.at[3]),
    ]

    def h_cols(p, core):
        return pl.ds(pl.multiple_of(p * 1024 + core * HALF, HALF), HALF)

    h_in = [
        pltpu.make_async_copy(hid.at[0, :, :, h_cols(p, c)], H.at[p, pl.ds(0, 2)], loc.at[4 + p])
        for p in range(8)
    ]
    for cp in w_in + h_in + others_in:
        cp.start()

    bar = pltpu.get_barrier_semaphore()
    near = (twin,) + y_to + z_to + x_to
    for d in near:
        pl.semaphore_signal(bar, inc=1, device_id=d, device_id_type=MESH)
    pl.semaphore_wait(bar, len(near))

    def tell(i, to):
        for d in to:
            pl.semaphore_signal(far.at[i], inc=1, device_id=d, device_id_type=MESH)

    def told(i):
        pl.semaphore_wait(far.at[i], 2)

    started = []

    def go(cp):
        cp.start()
        started.append(cp)

    h_out = [
        rc(hid.at[0, :, :, h_cols(p, 1 - c)], H.at[p, pl.ds(2, 2)], hs.at[p], hr.at[p], twin)
        for p in range(8)
    ]

    def piece(dz, dy):
        zz = zl if dz == 0 else 1 - zl
        return zz * 4 + (y + dy) % 4

    def rows_share(d, other=False):
        par = pa if d == 0 else pb
        if other:
            par = 1 - par
        base = 2 * COMMON + d * 2 * SHARE
        return pl.ds(pl.multiple_of(base + SHARE * par, 16), SHARE)

    def rows_common(d):
        return pl.ds(COMMON * d, COMMON)

    def y_msg(d, m, received):
        step = 1 - 2 * d
        back = 1 if m in (2, 4) else 0
        dy = -step * (back + (1 if received else 0))
        rows = {0: rows_share(d), 1: rows_common(d), 2: rows_share(d), 3: rows_share(1 - d),
                4: rows_common(d), 5: rows_common(1 - d)}[m]
        ref = W.at[piece(0, dy % 4), rows, :]
        return rc(ref, ref, ys.at[d, m], yr.at[d, m], y_to[d])

    def z_msg(d, dy, m, received):
        rows = rows_share(d) if m == 0 else rows_common(d)
        ref = W.at[piece(1 if received else 0, dy % 4), rows, :]
        return rc(ref, ref, zs.at[d, dy % 4, m], zr.at[d, dy % 4, m], z_to[d])

    def x_msg(d, dz, dy, received):
        ref = W.at[piece(dz, dy % 4), rows_share(d, received), :]
        i = dz * 4 + dy % 4
        return rc(ref, ref, xs.at[d, i], xr.at[d, i], x_to[d])

    def tokens(p, half):
        return H[p, pl.ds(half * 2, 2)].reshape(512, HALF)

    def mm(p, first, halves):
        for half in halves:
            for lo, n in ((0, 512), (512, 512), (1024, 128)):
                cols = pl.ds(lo, n)
                r = jnp.dot(tokens(p, half), W[p, :, cols], preferred_element_type=F32).reshape(2, 256, n)
                if first:
                    acc[pl.ds(half * 2, 2), :, cols] = r
                else:
                    acc[pl.ds(half * 2, 2), :, cols] += r

    def mm_last(half):
        p, q = piece(1, 1), piece(1, 3)

        @pl.loop(0, 3)
        def _(nb):
            cols = pl.ds(pl.multiple_of(nb * 384, 384), 384)
            r = jnp.dot(tokens(p, half), W[p, :, cols], preferred_element_type=F32)
            r += jnp.dot(tokens(q, half), W[q, :, cols], preferred_element_type=F32)
            r = r.reshape(2, 256, 384)
            if half:
                L[:, :, cols] = r.astype(BF16)
            else:
                acc[pl.ds(0, 2), :, cols] += r

    for cp in w_in:
        cp.wait()
    for d in range(2):
        go(y_msg(d, 0, False))
        go(z_msg(d, 0, 0, False))
    for p in range(4):
        go(h_out[p])
    for d in range(2):
        go(y_msg(d, 1, False))
        go(z_msg(d, 0, 1, False))
    for p in range(4, 8):
        go(h_out[p])

    tell(0, x_to)
    tell(1, y_to)
    for d in range(2):
        s = 1 - 2 * d
        y_msg(d, 0, True).wait_recv()
        go(y_msg(d, 2, False))
        go(y_msg(d, 3, False))
        go(z_msg(d, -s, 0, False))
        go(x_msg(d, 0, -s, False))
    for d in range(2):
        z_msg(d, 0, 0, True).wait_recv()
        go(x_msg(d, 1, 0, False))
    told(0)
    told(1)
    tell(2, z_to)
    for d in range(2):
        s = 1 - 2 * d
        y_msg(d, 1, True).wait_recv()
        go(y_msg(d, 4, False))
        go(y_msg(d, 5, False))
        go(z_msg(d, -s, 1, False))
    told(2)
    tell(3, z_to)
    for cp in h_in:
        cp.wait()
    for cp in h_out:
        cp.wait_recv()
    mm(piece(0, 0), True, (0, 1))
    for d in range(2):
        s = 1 - 2 * d
        y_msg(d, 2, True).wait_recv()
        go(z_msg(d, 2, 0, False))
        go(x_msg(d, 0, 2, False))
        z_msg(d, -s, 0, True).wait_recv()
        go(x_msg(d, 1, -s, False))
    for d in range(2):
        z_msg(d, 0, 1, True).wait_recv()
        x_msg(d, 1, 0, True).wait_recv()
    mm(piece(1, 0), False, (0, 1))
    told(3)
    tell(4, z_to)
    for d in range(2):
        s = 1 - 2 * d
        y_msg(1 - d, 3, True).wait_recv()
        go(z_msg(d, s, 0, False))
        go(x_msg(d, 0, s, False))
    told(4)
    tell(5, z_to)
    for d in range(2):
        y_msg(d, 4, True).wait_recv()
        go(z_msg(d, 2, 1, False))
        z_msg(d, 2, 0, True).wait_recv()
        go(x_msg(d, 1, 2, False))
    told(5)
    for d in range(2):
        s = 1 - 2 * d
        y_msg(1 - d, 5, True).wait_recv()
        go(z_msg(d, s, 1, False))
        z_msg(d, s, 0, True).wait_recv()
        go(x_msg(d, 1, s, False))
    for dy in (2, 1, 3):
        for d in range(2):
            x_msg(d, 0, dy, True).wait_recv()
        mm(piece(0, dy), False, (0, 1))
    for d in range(2):
        z_msg(d, 2, 1, True).wait_recv()
        x_msg(d, 1, 2, True).wait_recv()
    mm(piece(1, 2), False, (1,))
    early = rc(acc.at[pl.ds(2, 2)], R, ps.at[0], pr.at[0], twin)
    go(early)
    mm(piece(1, 2), False, (0,))
    for dy in (1, 3):
        for d in range(2):
            z_msg(d, dy, 1, True).wait_recv()
            x_msg(d, 1, dy, True).wait_recv()
    mm_last(1)
    late = rc(L, RL, ps.at[1], pr.at[1], twin)
    go(late)
    mm_last(0)
    for cp in others_in:
        cp.wait()
    early.wait_recv()
    late.wait_recv()

    for s in range(2):
        t = (acc[s, :, pl.ds(1024, 128)] + R[s, :, pl.ds(1024, 128)]
             + RL[s, :, pl.ds(1024, 128)].astype(F32)).astype(BF16)
        low[pl.ds(s * 256, 256), :] = t
        for i in range(2):
            pol[s, :, pl.ds(i * 512, 512)] = adapter_scale * jnp.dot(
                t[:, i * 64:(i + 1) * 64], up[i], preferred_element_type=F32)

    def token_weight(s, r):
        pos = r * 32 + lax.broadcasted_iota(jnp.int32, (32, 1), 0)
        sign = jnp.where(chosen[0] == s, 1.0, -1.0).astype(F32)
        return jnp.where(pos >= 256 - lengths[0, s], sign, 0.0)

    total = jnp.zeros((32, 512), F32)
    for s in range(2):
        def first_pass(r, total, s=s):
            rows = pl.ds(pl.multiple_of(r * 32, 32), 32)
            kr = acc[s, rows, pl.ds(0, 512)] + (
                R[s, rows, pl.ds(0, 512)] + RL[s, rows, pl.ds(0, 512)].astype(F32))
            vr = acc[s, rows, pl.ds(512, 512)] + (
                R[s, rows, pl.ds(512, 512)] + RL[s, rows, pl.ds(512, 512)].astype(F32))
            kp = kr + pol[s, rows, pl.ds(0, 512)]
            vp = vr + pol[s, rows, pl.ds(512, 512)]
            pol[s, rows, pl.ds(0, 512)] = kp
            pol[s, rows, pl.ds(512, 512)] = vp
            read = ro[s, rows, :].astype(F32)
            return total + token_weight(s, r) * (read * (kp * vp - kr * vr))
        total = lax.fori_loop(0, 8, first_pass, total)
    margin = jnp.sum(jnp.sum(total, axis=0, keepdims=True), axis=1, keepdims=True)
    pair_weight = -preference_beta * jax.nn.sigmoid(-preference_beta * margin)

    for s in range(2):
        def second_pass(r, carry, s=s):
            rows = pl.ds(pl.multiple_of(r * 32, 32), 32)
            whole = pl.ds(pl.multiple_of(s * 256 + r * 32, 32), 32)
            read = (pair_weight * token_weight(s, r)) * ro[s, rows, :].astype(F32)
            gk[whole, :] = (read * pol[s, rows, pl.ds(512, 512)]).astype(BF16)
            gv[whole, :] = (read * pol[s, rows, pl.ds(0, 512)]).astype(BF16)
            return carry
        lax.fori_loop(0, 8, second_pass, 0)

    nt = (((1,), (1,)), ((), ()))
    for i, g in enumerate((gk, gv)):
        BT[0, pl.ds(i * 64, 64), :] = (adapter_scale * lax.dot_general(
            up[i], g[...], nt, preferred_element_type=F32)).astype(BF16)
    b_cp = rc(BT.at[0], BT.at[1], ts.at[0], tr.at[0], twin)
    go(b_cp)
    low_t = jnp.transpose(low[...].astype(F32)).astype(BF16)
    for i, g in enumerate((gk, gv)):
        U[i] = adapter_scale * jnp.dot(
            low_t[i * 64:(i + 1) * 64, :], g[...], preferred_element_type=F32)
    u_cp = rc(U.at[1 - c], UT, ts.at[1], tr.at[1], twin)
    go(u_cp)
    b_cp.wait_recv()

    def grad(p):
        own = jnp.dot(BT[0], H[p, pl.ds(0, 2)].reshape(512, 512), preferred_element_type=F32)
        return own + jnp.dot(BT[1], H[p, pl.ds(2, 2)].reshape(512, 512), preferred_element_type=F32)

    zd = []
    for dy in (2, 1, 3, 0):
        D[dy] = grad(piece(1, dy)).astype(BF16)
        for d in range(2):
            h = pl.ds(d * 64, 64)
            cp = rc(D.at[dy, h], RZ.at[dy, h], us.at[dy, d], ur.at[dy, d], z_to[d])
            go(cp)
            zd.append((dy, cp))

    u_cp.wait_recv()
    chip = U[c] + UT[...]
    for j in range(16):
        r, q = j // 4, j % 4
        US1[j] = chip[r * 16:(r + 1) * 16, q * 128:(q + 1) * 128].astype(BF16)

    def spread16(src, dst, send, recv):
        def one(k, carry):
            j = (me16 + k) % 16
            rc(src(j), dst.at[me16], send.at[k], recv.at[k], peer16(k)).start()
            return carry
        lax.fori_loop(1, 16, one, 0)

    def land16(src, dst, send, recv):
        def one(k, carry):
            j = (me16 + 16 - k) % 16
            rc(src(j), dst.at[j], send.at[k], recv.at[k], peer16(k)).wait_recv()
            return carry
        lax.fori_loop(1, 16, one, 0)

    def sent16(src, dst, send, recv):
        def one(k, carry):
            j = (me16 + k) % 16
            rc(src(j), dst.at[me16], send.at[k], recv.at[k], peer16(k)).wait_send()
            return carry
        lax.fori_loop(1, 16, one, 0)

    u_args = (lambda j: US1.at[j], US2, vs, vr)
    spread16(*u_args)
    US2[me16] = US1[me16]

    for dy in (2, 1, 3, 0):
        E[dy] = grad(piece(0, dy))
    yd = []
    for dy in (2, 1, 3, 0):
        for dd, cp in zd:
            if dd == dy:
                cp.wait_recv()
        t = E[dy] + RZ[dy].astype(F32)
        if dy:
            D2[dy] = t.astype(BF16)
            cp = rc(D2.at[dy], RY.at[dy], qs.at[dy], qr.at[dy], at_y(dy))
            go(cp)
            yd.append(cp)
        else:
            E[0] = t

    land16(*u_args)
    UA[...] = jnp.sum(US2[...].astype(F32), axis=0).astype(BF16)
    UB[fs] = UA[...]
    for k in range(1, 8):
        go(rc(UA, UB.at[fs], ws.at[k], wr.at[k], peer8(k)))

    for cp in yd:
        cp.wait_recv()
    t = E[0] + RY[1].astype(F32) + RY[2].astype(F32) + RY[3].astype(F32)
    S1[...] = jnp.transpose(t).astype(BF16).reshape(16, 32, 128)
    s_args = (lambda j: S1.at[j], S2, ss, sr)
    spread16(*s_args)
    S2[me16] = S1[me16]
    for k in range(1, 8):
        rc(UA, UB.at[(fs + 8 - k) % 8], ws.at[k], wr.at[k], peer8(k)).wait_recv()
    GU[c, me16] = jnp.sum(UB[...].astype(F32), axis=0).astype(BF16)
    gu_args = (lambda j: GU.at[c, me16], GU.at[c], es, er)
    spread16(*gu_args)
    land16(*s_args)
    GD[c, me16] = jnp.sum(S2[...].astype(F32), axis=0).astype(BF16)
    gd_args = (lambda j: GD.at[c, me16], GD.at[c], gs, gr)
    spread16(*gd_args)
    land16(*gu_args)
    land16(*gd_args)
    out = [rc(GD.at[c], GD.at[c], ts.at[2], tr.at[2], twin), rc(GU.at[c], GU.at[c], ts.at[3], tr.at[3], twin)]
    for cp in out:
        go(cp)
    for cp in out:
        cp.wait_recv()
    for cp in started:
        cp.wait_send()
    for args in (u_args, s_args, gu_args, gd_args):
        sent16(*args)


def widen(gd, gu, od, ou):
    od[...] = gd[...].astype(F32).reshape(1024, 128)
    for core in range(2):
        for j in range(16):
            ou[core, pl.ds((j // 4) * 16, 16), pl.ds((j % 4) * 128, 128)] = gu[core, j].astype(F32)


def local(hidden, frozen_weight, adapter_down_weight, adapter_up_weight, readout, chosen, response_length):
    dma = pltpu.SemaphoreType.DMA
    vmem = pltpu.VMEM
    anywhere = pl.BlockSpec(memory_space=pl.ANY)
    smem = pl.BlockSpec(memory_space=pltpu.SMEM)
    gd, gu = pl.pallas_call(
        kernel,
        out_shape=(
            jax.ShapeDtypeStruct((2, 16, 32, 128), BF16),
            jax.ShapeDtypeStruct((2, 16, 16, 128), BF16),
        ),
        in_specs=[anywhere] * 5 + [smem] * 2,
        out_specs=(pl.BlockSpec(memory_space=pltpu.VMEM), pl.BlockSpec(memory_space=pltpu.VMEM)),
        scratch_shapes=[
            vmem((8, HALF, WIDE), BF16),
            vmem((8, 4, 256, HALF), BF16),
            vmem((4, 256, WIDE), F32),
            vmem((2, 256, WIDE), F32),
            vmem((2, 256, WIDE), BF16),
            vmem((2, 256, WIDE), BF16),
            vmem((2, 64, 512), BF16),
            vmem((2, 256, 512), BF16),
            vmem((2, 256, 1024), F32),
            vmem((512, 128), BF16),
            vmem((512, 512), BF16),
            vmem((512, 512), BF16),
            vmem((2, 128, 512), BF16),
            vmem((2, 64, 512), F32),
            vmem((64, 512), F32),
            vmem((16, 16, 128), BF16),
            vmem((16, 16, 128), BF16),
            vmem((16, 128), BF16),
            vmem((8, 16, 128), BF16),
            vmem((4, 128, 512), BF16),
            vmem((4, 128, 512), BF16),
            vmem((4, 128, 512), F32),
            vmem((4, 128, 512), BF16),
            vmem((4, 128, 512), BF16),
            vmem((16, 32, 128), BF16),
            vmem((16, 32, 128), BF16),
            dma((12,)),
            dma((8,)), dma((8,)),
            dma((2, 6)), dma((2, 6)),
            dma((2, 4, 2)), dma((2, 4, 2)),
            dma((2, 8)), dma((2, 8)),
            dma((2,)), dma((2,)),
            dma((4,)), dma((4,)),
            dma((4, 2)), dma((4, 2)),
            dma((16,)), dma((16,)),
            dma((4,)), dma((4,)),
            dma((8,)), dma((8,)),
            dma((16,)), dma((16,)),
            dma((16,)), dma((16,)),
            dma((16,)), dma((16,)),
            pltpu.SemaphoreType.REGULAR((6,)),
        ],
        compiler_params=pltpu.CompilerParams(
            collective_id=0, has_side_effects=True, vmem_limit_bytes=56 * 2**20
        ),
        cost_estimate=pl.CostEstimate(flops=12 * 10**9, bytes_accessed=12 * 10**6, transcendentals=1),
    )(hidden, frozen_weight, adapter_down_weight, adapter_up_weight, readout, chosen, response_length)
    return pl.pallas_call(
        widen,
        out_shape=(
            jax.ShapeDtypeStruct((1024, 128), F32),
            jax.ShapeDtypeStruct((2, 64, 512), F32),
        ),
        in_specs=[pl.BlockSpec(memory_space=pltpu.VMEM)] * 2,
        out_specs=(pl.BlockSpec(memory_space=pltpu.VMEM),) * 2,
        cost_estimate=pl.CostEstimate(flops=10**6, bytes_accessed=2 * 10**6, transcendentals=0),
    )(gd, gu)


def solution(mesh):
    placed = (
        P(("dp", "fsdp"), None, None, None),
        P("fsdp", None),
        P("fsdp", None),
        P(),
        P(("dp", "fsdp"), None, None, None),
        P(("dp", "fsdp")),
        P(("dp", "fsdp"), None),
    )
    return jax.shard_map(
        local, mesh=mesh, in_specs=placed, out_specs=(P("fsdp", None), P()), check_vma=False
    )
```

```python
import jax
import jax.numpy as jnp
from jax import lax
from jax.experimental import pallas as pl
from jax.experimental.pallas import tpu as pltpu
from jax.sharding import PartitionSpec as P

MESH = pl.DeviceIdType.MESH
F32 = jnp.float32
BF16 = jnp.bfloat16
adapter_scale = 0.5
preference_beta = 0.1

HALF = 512
COMMON = 96
SHARE = 80
WIDE = 1152


def kernel(
    hid, fw, ad, up_h, ro_h, chosen, lengths, GD, GU,
    W, H, acc, R, L, RL, up, ro, pol, low, gk, gv, BT, U, UT, US1, US2, UA, UB,
    D, RZ, E, D2, RY, S1, S2,
    loc, hs, hr, ys, yr, zs, zr, xs, xr, ps, pr, ts, tr, us, ur, vs, vr, qs, qr, ws, wr, ss, sr, gs, gr, es, er, far,
):
    dp = lax.axis_index("dp")
    fs = lax.axis_index("fsdp")
    zh, x, c = dp // 8, (dp // 2) % 4, dp % 2
    zl, y = fs // 4, fs % 4
    me16 = dp // 2
    z = zh * 2 + zl

    def dev(zh_, x_, c_, zl_, y_):
        return ((zh_ * 4 + x_) * 2 + c_, zl_ * 4 + y_)

    def at_y(n):
        return dev(zh, x, c, zl, (y + n + 4) % 4)

    def at_z(n):
        zz = (z + n + 8) % 8
        return dev(zz // 2, x, c, zz % 2, y)

    twin = dev(zh, x, 1 - c, zl, y)
    pa, pb = x % 2, x // 2
    x_a = dev(zh, x + 1 - 2 * pa, c, zl, y)
    x_b = dev(zh, (x + 3 + 2 * pa) % 4, c, zl, y)
    y_to = (at_y(1), at_y(-1))
    z_to = (at_z(1), at_z(-1))
    x_to = (x_a, x_b)

    def peer16(k):
        j = (me16 + k) % 16
        return (j * 2 + c, fs)

    def peer8(k):
        return (dp, (fs + k) % 8)

    def rc(src, dst, s, r, d):
        return pltpu.make_async_remote_copy(
            src_ref=src, dst_ref=dst, send_sem=s, recv_sem=r, device_id=d, device_id_type=MESH
        )

    mine = fs
    w_in = [
        pltpu.make_async_copy(
            fw.at[pl.ds(pl.multiple_of(c * HALF, HALF), HALF), :],
            W.at[mine, :, pl.ds(0, 1024)], loc.at[0]),
        pltpu.make_async_copy(
            ad.at[pl.ds(pl.multiple_of(c * HALF, HALF), HALF), :],
            W.at[mine, :, pl.ds(1024, 128)], loc.at[1]),
    ]
    others_in = [
        pltpu.make_async_copy(ro_h.at[0], ro, loc.at[2]),
        pltpu.make_async_copy(up_h, up, loc.at[3]),
    ]

    def h_cols(p, core):
        return pl.ds(pl.multiple_of(p * 1024 + core * HALF, HALF), HALF)

    h_in = [
        pltpu.make_async_copy(hid.at[0, :, :, h_cols(p, c)], H.at[p, pl.ds(0, 2)], loc.at[4 + p])
        for p in range(8)
    ]
    for cp in w_in + h_in + others_in:
        cp.start()

    bar = pltpu.get_barrier_semaphore()
    near = (twin,) + y_to + z_to + x_to
    for d in near:
        pl.semaphore_signal(bar, inc=1, device_id=d, device_id_type=MESH)
    pl.semaphore_wait(bar, len(near))

    def tell(i, to):
        for d in to:
            pl.semaphore_signal(far.at[i], inc=1, device_id=d, device_id_type=MESH)

    def told(i):
        pl.semaphore_wait(far.at[i], 2)

    started = []

    def go(cp):
        cp.start()
        started.append(cp)

    h_out = [
        rc(hid.at[0, :, :, h_cols(p, 1 - c)], H.at[p, pl.ds(2, 2)], hs.at[p], hr.at[p], twin)
        for p in range(8)
    ]

    def piece(dz, dy):
        zz = zl if dz == 0 else 1 - zl
        return zz * 4 + (y + dy) % 4

    def rows_share(d, other=False):
        par = pa if d == 0 else pb
        if other:
            par = 1 - par
        base = 2 * COMMON + d * 2 * SHARE
        return pl.ds(pl.multiple_of(base + SHARE * par, 16), SHARE)

    def rows_common(d):
        return pl.ds(COMMON * d, COMMON)

    def y_msg(d, m, received):
        step = 1 - 2 * d
        back = 1 if m in (2, 4) else 0
        dy = -step * (back + (1 if received else 0))
        rows = {0: rows_share(d), 1: rows_common(d), 2: rows_share(d), 3: rows_share(1 - d),
                4: rows_common(d), 5: rows_common(1 - d)}[m]
        ref = W.at[piece(0, dy % 4), rows, :]
        return rc(ref, ref, ys.at[d, m], yr.at[d, m], y_to[d])

    def z_msg(d, dy, m, received):
        rows = rows_share(d) if m == 0 else rows_common(d)
        ref = W.at[piece(1 if received else 0, dy % 4), rows, :]
        return rc(ref, ref, zs.at[d, dy % 4, m], zr.at[d, dy % 4, m], z_to[d])

    def x_msg(d, dz, dy, received):
        ref = W.at[piece(dz, dy % 4), rows_share(d, received), :]
        i = dz * 4 + dy % 4
        return rc(ref, ref, xs.at[d, i], xr.at[d, i], x_to[d])

    def tokens(p, half):
        return H[p, pl.ds(half * 2, 2)].reshape(512, HALF)

    def mm(p, first, halves):
        for half in halves:
            for lo, n in ((0, 512), (512, 512), (1024, 128)):
                cols = pl.ds(lo, n)
                r = jnp.dot(tokens(p, half), W[p, :, cols], preferred_element_type=F32).reshape(2, 256, n)
                if first:
                    acc[pl.ds(half * 2, 2), :, cols] = r
                else:
                    acc[pl.ds(half * 2, 2), :, cols] += r

    def mm_last(half):
        p, q = piece(1, 1), piece(1, 3)

        @pl.loop(0, 3)
        def _(nb):
            cols = pl.ds(pl.multiple_of(nb * 384, 384), 384)
            r = jnp.dot(tokens(p, half), W[p, :, cols], preferred_element_type=F32)
            r += jnp.dot(tokens(q, half), W[q, :, cols], preferred_element_type=F32)
            r = r.reshape(2, 256, 384)
            if half:
                L[:, :, cols] = r.astype(BF16)
            else:
                acc[pl.ds(0, 2), :, cols] += r

    for cp in w_in:
        cp.wait()
    for d in range(2):
        go(y_msg(d, 0, False))
        go(z_msg(d, 0, 0, False))
    for p in range(4):
        go(h_out[p])
    for d in range(2):
        go(y_msg(d, 1, False))
        go(z_msg(d, 0, 1, False))
    for p in range(4, 8):
        go(h_out[p])

    tell(0, x_to)
    tell(1, y_to)
    for d in range(2):
        s = 1 - 2 * d
        y_msg(d, 0, True).wait_recv()
        go(y_msg(d, 2, False))
        go(y_msg(d, 3, False))
        go(z_msg(d, -s, 0, False))
        go(x_msg(d, 0, -s, False))
    for d in range(2):
        z_msg(d, 0, 0, True).wait_recv()
        go(x_msg(d, 1, 0, False))
    told(0)
    told(1)
    tell(2, z_to)
    for d in range(2):
        s = 1 - 2 * d
        y_msg(d, 1, True).wait_recv()
        go(y_msg(d, 4, False))
        go(y_msg(d, 5, False))
        go(z_msg(d, -s, 1, False))
    told(2)
    tell(3, z_to)
    for cp in h_in:
        cp.wait()
    for cp in h_out:
        cp.wait_recv()
    mm(piece(0, 0), True, (0, 1))
    for d in range(2):
        s = 1 - 2 * d
        y_msg(d, 2, True).wait_recv()
        go(z_msg(d, 2, 0, False))
        go(x_msg(d, 0, 2, False))
        z_msg(d, -s, 0, True).wait_recv()
        go(x_msg(d, 1, -s, False))
    for d in range(2):
        z_msg(d, 0, 1, True).wait_recv()
        x_msg(d, 1, 0, True).wait_recv()
    mm(piece(1, 0), False, (0, 1))
    told(3)
    tell(4, z_to)
    for d in range(2):
        s = 1 - 2 * d
        y_msg(1 - d, 3, True).wait_recv()
        go(z_msg(d, s, 0, False))
        go(x_msg(d, 0, s, False))
    told(4)
    tell(5, z_to)
    for d in range(2):
        y_msg(d, 4, True).wait_recv()
        go(z_msg(d, 2, 1, False))
        z_msg(d, 2, 0, True).wait_recv()
        go(x_msg(d, 1, 2, False))
    told(5)
    for d in range(2):
        s = 1 - 2 * d
        y_msg(1 - d, 5, True).wait_recv()
        go(z_msg(d, s, 1, False))
        z_msg(d, s, 0, True).wait_recv()
        go(x_msg(d, 1, s, False))
    for dy in (2, 1, 3):
        for d in range(2):
            x_msg(d, 0, dy, True).wait_recv()
        mm(piece(0, dy), False, (0, 1))
    for d in range(2):
        z_msg(d, 2, 1, True).wait_recv()
        x_msg(d, 1, 2, True).wait_recv()
    mm(piece(1, 2), False, (1,))
    early = rc(acc.at[pl.ds(2, 2)], R, ps.at[0], pr.at[0], twin)
    go(early)
    mm(piece(1, 2), False, (0,))
    for dy in (1, 3):
        for d in range(2):
            z_msg(d, dy, 1, True).wait_recv()
            x_msg(d, 1, dy, True).wait_recv()
    mm_last(1)
    late = rc(L, RL, ps.at[1], pr.at[1], twin)
    go(late)
    mm_last(0)
    for cp in others_in:
        cp.wait()
    early.wait_recv()
    late.wait_recv()

    for s in range(2):
        t = (acc[s, :, pl.ds(1024, 128)] + R[s, :, pl.ds(1024, 128)]
             + RL[s, :, pl.ds(1024, 128)].astype(F32)).astype(BF16)
        low[pl.ds(s * 256, 256), :] = t
        for i in range(2):
            pol[s, :, pl.ds(i * 512, 512)] = adapter_scale * jnp.dot(
                t[:, i * 64:(i + 1) * 64], up[i], preferred_element_type=F32)

    def token_weight(s, r):
        pos = r * 32 + lax.broadcasted_iota(jnp.int32, (32, 1), 0)
        sign = jnp.where(chosen[0] == s, 1.0, -1.0).astype(F32)
        return jnp.where(pos >= 256 - lengths[0, s], sign, 0.0)

    total = jnp.zeros((32, 512), F32)
    for s in range(2):
        def first_pass(r, total, s=s):
            rows = pl.ds(pl.multiple_of(r * 32, 32), 32)
            kr = acc[s, rows, pl.ds(0, 512)] + (
                R[s, rows, pl.ds(0, 512)] + RL[s, rows, pl.ds(0, 512)].astype(F32))
            vr = acc[s, rows, pl.ds(512, 512)] + (
                R[s, rows, pl.ds(512, 512)] + RL[s, rows, pl.ds(512, 512)].astype(F32))
            kp = kr + pol[s, rows, pl.ds(0, 512)]
            vp = vr + pol[s, rows, pl.ds(512, 512)]
            pol[s, rows, pl.ds(0, 512)] = kp
            pol[s, rows, pl.ds(512, 512)] = vp
            read = ro[s, rows, :].astype(F32)
            return total + token_weight(s, r) * (read * (kp * vp - kr * vr))
        total = lax.fori_loop(0, 8, first_pass, total)
    margin = jnp.sum(jnp.sum(total, axis=0, keepdims=True), axis=1, keepdims=True)
    pair_weight = -preference_beta * jax.nn.sigmoid(-preference_beta * margin)

    for s in range(2):
        def second_pass(r, carry, s=s):
            rows = pl.ds(pl.multiple_of(r * 32, 32), 32)
            whole = pl.ds(pl.multiple_of(s * 256 + r * 32, 32), 32)
            read = (pair_weight * token_weight(s, r)) * ro[s, rows, :].astype(F32)
            gk[whole, :] = (read * pol[s, rows, pl.ds(512, 512)]).astype(BF16)
            gv[whole, :] = (read * pol[s, rows, pl.ds(0, 512)]).astype(BF16)
            return carry
        lax.fori_loop(0, 8, second_pass, 0)

    nt = (((1,), (1,)), ((), ()))
    for i, g in enumerate((gk, gv)):
        BT[0, pl.ds(i * 64, 64), :] = (adapter_scale * lax.dot_general(
            up[i], g[...], nt, preferred_element_type=F32)).astype(BF16)
    b_cp = rc(BT.at[0], BT.at[1], ts.at[0], tr.at[0], twin)
    go(b_cp)
    low_t = jnp.transpose(low[...].astype(F32)).astype(BF16)
    for i, g in enumerate((gk, gv)):
        U[i] = adapter_scale * jnp.dot(
            low_t[i * 64:(i + 1) * 64, :], g[...], preferred_element_type=F32)
    u_cp = rc(U.at[1 - c], UT, ts.at[1], tr.at[1], twin)
    go(u_cp)
    b_cp.wait_recv()

    def grad(p):
        own = jnp.dot(BT[0], H[p, pl.ds(0, 2)].reshape(512, 512), preferred_element_type=F32)
        return own + jnp.dot(BT[1], H[p, pl.ds(2, 2)].reshape(512, 512), preferred_element_type=F32)

    zd = []
    for dy in (2, 1, 3, 0):
        D[dy] = grad(piece(1, dy)).astype(BF16)
        for d in range(2):
            h = pl.ds(d * 64, 64)
            cp = rc(D.at[dy, h], RZ.at[dy, h], us.at[dy, d], ur.at[dy, d], z_to[d])
            go(cp)
            zd.append((dy, cp))

    u_cp.wait_recv()
    chip = U[c] + UT[...]
    for j in range(16):
        r, q = j // 4, j % 4
        US1[j] = chip[r * 16:(r + 1) * 16, q * 128:(q + 1) * 128].astype(BF16)

    def spread16(src, dst, send, recv):
        for k in (10, 9, 11, 8, 6, 14, 5, 13, 7, 15, 4, 12, 2, 1, 3):
            j = (me16 + k) % 16
            rc(src(j), dst.at[me16], send.at[k], recv.at[k], peer16(k)).start()

    def land16(src, dst, send, recv):
        def one(k, carry):
            j = (me16 + 16 - k) % 16
            rc(src(j), dst.at[j], send.at[k], recv.at[k], peer16(k)).wait_recv()
            return carry
        lax.fori_loop(1, 16, one, 0, unroll=True)

    def sent16(src, dst, send, recv):
        def one(k, carry):
            j = (me16 + k) % 16
            rc(src(j), dst.at[me16], send.at[k], recv.at[k], peer16(k)).wait_send()
            return carry
        lax.fori_loop(1, 16, one, 0, unroll=True)

    u_args = (lambda j: US1.at[j], US2, vs, vr)
    spread16(*u_args)
    US2[me16] = US1[me16]

    for dy in (2, 1, 3, 0):
        E[dy] = grad(piece(0, dy))
    yd = []
    for dy in (2, 1, 3, 0):
        for dd, cp in zd:
            if dd == dy:
                cp.wait_recv()
        t = E[dy] + RZ[dy].astype(F32)
        if dy:
            D2[dy] = t.astype(BF16)
            cp = rc(D2.at[dy], RY.at[dy], qs.at[dy], qr.at[dy], at_y(dy))
            go(cp)
            yd.append(cp)
        else:
            E[0] = t

    land16(*u_args)
    UA[...] = jnp.sum(US2[...].astype(F32), axis=0).astype(BF16)
    UB[fs] = UA[...]
    for k in range(1, 8):
        go(rc(UA, UB.at[fs], ws.at[k], wr.at[k], peer8(k)))

    for cp in yd:
        cp.wait_recv()
    t = E[0] + RY[1].astype(F32) + RY[2].astype(F32) + RY[3].astype(F32)
    S1[...] = jnp.transpose(t).astype(BF16).reshape(16, 32, 128)
    s_args = (lambda j: S1.at[j], S2, ss, sr)
    spread16(*s_args)
    S2[me16] = S1[me16]
    for k in range(1, 8):
        rc(UA, UB.at[(fs + 8 - k) % 8], ws.at[k], wr.at[k], peer8(k)).wait_recv()
    GU[c, me16] = jnp.sum(UB[...].astype(F32), axis=0).astype(BF16)
    gu_args = (lambda j: GU.at[c, me16], GU.at[c], es, er)
    spread16(*gu_args)
    land16(*s_args)
    GD[c, me16] = jnp.sum(S2[...].astype(F32), axis=0).astype(BF16)
    gd_args = (lambda j: GD.at[c, me16], GD.at[c], gs, gr)
    spread16(*gd_args)
    land16(*gu_args)
    go(rc(GU.at[c], GU.at[c], ts.at[3], tr.at[3], twin))
    land16(*gd_args)
    out = [rc(GU.at[c], GU.at[c], ts.at[3], tr.at[3], twin), rc(GD.at[c], GD.at[c], ts.at[2], tr.at[2], twin)]
    go(out[1])
    for cp in out:
        cp.wait_recv()
    for cp in started:
        cp.wait_send()
    for args in (u_args, s_args, gu_args, gd_args):
        sent16(*args)


def widen(gd, gu, od, ou):
    od[...] = gd[...].astype(F32).reshape(1024, 128)
    for core in range(2):
        for j in range(16):
            ou[core, pl.ds((j // 4) * 16, 16), pl.ds((j % 4) * 128, 128)] = gu[core, j].astype(F32)


def local(hidden, frozen_weight, adapter_down_weight, adapter_up_weight, readout, chosen, response_length):
    dma = pltpu.SemaphoreType.DMA
    vmem = pltpu.VMEM
    anywhere = pl.BlockSpec(memory_space=pl.ANY)
    smem = pl.BlockSpec(memory_space=pltpu.SMEM)
    gd, gu = pl.pallas_call(
        kernel,
        out_shape=(
            jax.ShapeDtypeStruct((2, 16, 32, 128), BF16),
            jax.ShapeDtypeStruct((2, 16, 16, 128), BF16),
        ),
        in_specs=[anywhere] * 5 + [smem] * 2,
        out_specs=(pl.BlockSpec(memory_space=pltpu.VMEM), pl.BlockSpec(memory_space=pltpu.VMEM)),
        scratch_shapes=[
            vmem((8, HALF, WIDE), BF16),
            vmem((8, 4, 256, HALF), BF16),
            vmem((4, 256, WIDE), F32),
            vmem((2, 256, WIDE), F32),
            vmem((2, 256, WIDE), BF16),
            vmem((2, 256, WIDE), BF16),
            vmem((2, 64, 512), BF16),
            vmem((2, 256, 512), BF16),
            vmem((2, 256, 1024), F32),
            vmem((512, 128), BF16),
            vmem((512, 512), BF16),
            vmem((512, 512), BF16),
            vmem((2, 128, 512), BF16),
            vmem((2, 64, 512), F32),
            vmem((64, 512), F32),
            vmem((16, 16, 128), BF16),
            vmem((16, 16, 128), BF16),
            vmem((16, 128), BF16),
            vmem((8, 16, 128), BF16),
            vmem((4, 128, 512), BF16),
            vmem((4, 128, 512), BF16),
            vmem((4, 128, 512), F32),
            vmem((4, 128, 512), BF16),
            vmem((4, 128, 512), BF16),
            vmem((16, 32, 128), BF16),
            vmem((16, 32, 128), BF16),
            dma((12,)),
            dma((8,)), dma((8,)),
            dma((2, 6)), dma((2, 6)),
            dma((2, 4, 2)), dma((2, 4, 2)),
            dma((2, 8)), dma((2, 8)),
            dma((2,)), dma((2,)),
            dma((4,)), dma((4,)),
            dma((4, 2)), dma((4, 2)),
            dma((16,)), dma((16,)),
            dma((4,)), dma((4,)),
            dma((8,)), dma((8,)),
            dma((16,)), dma((16,)),
            dma((16,)), dma((16,)),
            dma((16,)), dma((16,)),
            pltpu.SemaphoreType.REGULAR((6,)),
        ],
        compiler_params=pltpu.CompilerParams(
            collective_id=0, has_side_effects=True, vmem_limit_bytes=56 * 2**20
        ),
        cost_estimate=pl.CostEstimate(flops=12 * 10**9, bytes_accessed=12 * 10**6, transcendentals=1),
    )(hidden, frozen_weight, adapter_down_weight, adapter_up_weight, readout, chosen, response_length)
    return pl.pallas_call(
        widen,
        out_shape=(
            jax.ShapeDtypeStruct((1024, 128), F32),
            jax.ShapeDtypeStruct((2, 64, 512), F32),
        ),
        in_specs=[pl.BlockSpec(memory_space=pltpu.VMEM)] * 2,
        out_specs=(pl.BlockSpec(memory_space=pltpu.VMEM),) * 2,
        cost_estimate=pl.CostEstimate(flops=10**6, bytes_accessed=2 * 10**6, transcendentals=0),
    )(gd, gu)


def solution(mesh):
    placed = (
        P(("dp", "fsdp"), None, None, None),
        P("fsdp", None),
        P("fsdp", None),
        P(),
        P(("dp", "fsdp"), None, None, None),
        P(("dp", "fsdp")),
        P(("dp", "fsdp"), None),
    )
    return jax.shard_map(
        local, mesh=mesh, in_specs=placed, out_specs=(P("fsdp", None), P()), check_vma=False
    )
```

```python
import jax
import jax.numpy as jnp
from jax import lax
from jax.experimental import pallas as pl
from jax.experimental.pallas import tpu as pltpu
from jax.sharding import PartitionSpec as P

MESH = pl.DeviceIdType.MESH
F32 = jnp.float32
BF16 = jnp.bfloat16
adapter_scale = 0.5
preference_beta = 0.1

HALF = 512
COMMON = 96
SHARE = 80
WIDE = 1152


def kernel(
    hid, fw, ad, up_h, ro_h, chosen, lengths, GD, GU,
    W, H, acc, R, L, RL, up, ro, pol, low, gk, gv, BT, U, UT, US1, US2, UA, UB,
    D, RZ, E, D2, RY, S1, S2,
    loc, hs, hr, ys, yr, zs, zr, xs, xr, ps, pr, ts, tr, us, ur, vs, vr, qs, qr, ws, wr, ss, sr, gs, gr, es, er, far,
):
    dp = lax.axis_index("dp")
    fs = lax.axis_index("fsdp")
    zh, x, c = dp // 8, (dp // 2) % 4, dp % 2
    zl, y = fs // 4, fs % 4
    me16 = dp // 2
    z = zh * 2 + zl

    def dev(zh_, x_, c_, zl_, y_):
        return ((zh_ * 4 + x_) * 2 + c_, zl_ * 4 + y_)

    def at_y(n):
        return dev(zh, x, c, zl, (y + n + 4) % 4)

    def at_z(n):
        zz = (z + n + 8) % 8
        return dev(zz // 2, x, c, zz % 2, y)

    twin = dev(zh, x, 1 - c, zl, y)
    pa, pb = x % 2, x // 2
    x_a = dev(zh, x + 1 - 2 * pa, c, zl, y)
    x_b = dev(zh, (x + 3 + 2 * pa) % 4, c, zl, y)
    y_to = (at_y(1), at_y(-1))
    z_to = (at_z(1), at_z(-1))
    x_to = (x_a, x_b)

    def peer16(k):
        j = (me16 + k) % 16
        return (j * 2 + c, fs)

    def peer8(k):
        return (dp, (fs + k) % 8)

    def rc(src, dst, s, r, d):
        return pltpu.make_async_remote_copy(
            src_ref=src, dst_ref=dst, send_sem=s, recv_sem=r, device_id=d, device_id_type=MESH
        )

    mine = fs
    w_in = [
        pltpu.make_async_copy(
            fw.at[pl.ds(pl.multiple_of(c * HALF, HALF), HALF), :],
            W.at[mine, :, pl.ds(0, 1024)], loc.at[0]),
        pltpu.make_async_copy(
            ad.at[pl.ds(pl.multiple_of(c * HALF, HALF), HALF), :],
            W.at[mine, :, pl.ds(1024, 128)], loc.at[1]),
    ]
    others_in = [
        pltpu.make_async_copy(ro_h.at[0], ro, loc.at[2]),
        pltpu.make_async_copy(up_h, up, loc.at[3]),
    ]

    def h_cols(p, core):
        return pl.ds(pl.multiple_of(p * 1024 + core * HALF, HALF), HALF)

    h_in = [
        pltpu.make_async_copy(hid.at[0, :, :, h_cols(p, c)], H.at[p, pl.ds(0, 2)], loc.at[4 + p])
        for p in range(8)
    ]
    for cp in w_in + h_in + others_in:
        cp.start()

    bar = pltpu.get_barrier_semaphore()
    near = (twin,) + y_to + z_to + x_to
    for d in near:
        pl.semaphore_signal(bar, inc=1, device_id=d, device_id_type=MESH)
    pl.semaphore_wait(bar, len(near))

    def tell(i, to):
        for d in to:
            pl.semaphore_signal(far.at[i], inc=1, device_id=d, device_id_type=MESH)

    def told(i):
        pl.semaphore_wait(far.at[i], 2)

    started = []

    def go(cp):
        cp.start()
        started.append(cp)

    h_out = [
        rc(hid.at[0, :, :, h_cols(p, 1 - c)], H.at[p, pl.ds(2, 2)], hs.at[p], hr.at[p], twin)
        for p in range(8)
    ]

    def piece(dz, dy):
        zz = zl if dz == 0 else 1 - zl
        return zz * 4 + (y + dy) % 4

    def rows_share(d, other=False):
        par = pa if d == 0 else pb
        if other:
            par = 1 - par
        base = 2 * COMMON + d * 2 * SHARE
        return pl.ds(pl.multiple_of(base + SHARE * par, 16), SHARE)

    def rows_common(d):
        return pl.ds(COMMON * d, COMMON)

    def y_msg(d, m, received):
        step = 1 - 2 * d
        back = 1 if m in (2, 4) else 0
        dy = -step * (back + (1 if received else 0))
        rows = {0: rows_share(d), 1: rows_common(d), 2: rows_share(d), 3: rows_share(1 - d),
                4: rows_common(d), 5: rows_common(1 - d)}[m]
        ref = W.at[piece(0, dy % 4), rows, :]
        return rc(ref, ref, ys.at[d, m], yr.at[d, m], y_to[d])

    def z_msg(d, dy, m, received):
        rows = rows_share(d) if m == 0 else rows_common(d)
        ref = W.at[piece(1 if received else 0, dy % 4), rows, :]
        return rc(ref, ref, zs.at[d, dy % 4, m], zr.at[d, dy % 4, m], z_to[d])

    def x_msg(d, dz, dy, received):
        ref = W.at[piece(dz, dy % 4), rows_share(d, received), :]
        i = dz * 4 + dy % 4
        return rc(ref, ref, xs.at[d, i], xr.at[d, i], x_to[d])

    def tokens(p, half):
        return H[p, pl.ds(half * 2, 2)].reshape(512, HALF)

    def mm(p, first, halves):
        for half in halves:
            for lo, n in ((0, 512), (512, 512), (1024, 128)):
                cols = pl.ds(lo, n)
                r = jnp.dot(tokens(p, half), W[p, :, cols], preferred_element_type=F32).reshape(2, 256, n)
                if first:
                    acc[pl.ds(half * 2, 2), :, cols] = r
                else:
                    acc[pl.ds(half * 2, 2), :, cols] += r

    def mm_last(half):
        p, q = piece(1, 1), piece(1, 3)

        @pl.loop(0, 3)
        def _(nb):
            cols = pl.ds(pl.multiple_of(nb * 384, 384), 384)
            r = jnp.dot(tokens(p, half), W[p, :, cols], preferred_element_type=F32)
            r += jnp.dot(tokens(q, half), W[q, :, cols], preferred_element_type=F32)
            r = r.reshape(2, 256, 384)
            if half:
                L[:, :, cols] = r.astype(BF16)
            else:
                acc[pl.ds(0, 2), :, cols] += r

    for cp in w_in:
        cp.wait()
    for d in range(2):
        go(y_msg(d, 0, False))
        go(z_msg(d, 0, 0, False))
    for p in range(4):
        go(h_out[p])
    for d in range(2):
        go(y_msg(d, 1, False))
        go(z_msg(d, 0, 1, False))
    for p in range(4, 8):
        go(h_out[p])

    tell(0, x_to)
    tell(1, y_to)
    for d in range(2):
        s = 1 - 2 * d
        y_msg(d, 0, True).wait_recv()
        go(y_msg(d, 2, False))
        go(y_msg(d, 3, False))
        go(z_msg(d, -s, 0, False))
        go(x_msg(d, 0, -s, False))
    for d in range(2):
        z_msg(d, 0, 0, True).wait_recv()
        go(x_msg(d, 1, 0, False))
    told(0)
    told(1)
    tell(2, z_to)
    for d in range(2):
        s = 1 - 2 * d
        y_msg(d, 1, True).wait_recv()
        go(y_msg(d, 4, False))
        go(y_msg(d, 5, False))
        go(z_msg(d, -s, 1, False))
    told(2)
    tell(3, z_to)
    for cp in h_in:
        cp.wait()
    for cp in h_out:
        cp.wait_recv()
    mm(piece(0, 0), True, (0, 1))
    for d in range(2):
        s = 1 - 2 * d
        y_msg(d, 2, True).wait_recv()
        go(z_msg(d, 2, 0, False))
        go(x_msg(d, 0, 2, False))
        z_msg(d, -s, 0, True).wait_recv()
        go(x_msg(d, 1, -s, False))
    for d in range(2):
        z_msg(d, 0, 1, True).wait_recv()
        x_msg(d, 1, 0, True).wait_recv()
    mm(piece(1, 0), False, (0, 1))
    told(3)
    tell(4, z_to)
    for d in range(2):
        s = 1 - 2 * d
        y_msg(1 - d, 3, True).wait_recv()
        go(z_msg(d, s, 0, False))
        go(x_msg(d, 0, s, False))
    told(4)
    tell(5, z_to)
    for d in range(2):
        y_msg(d, 4, True).wait_recv()
        go(z_msg(d, 2, 1, False))
        z_msg(d, 2, 0, True).wait_recv()
        go(x_msg(d, 1, 2, False))
    told(5)
    for d in range(2):
        s = 1 - 2 * d
        y_msg(1 - d, 5, True).wait_recv()
        go(z_msg(d, s, 1, False))
        z_msg(d, s, 0, True).wait_recv()
        go(x_msg(d, 1, s, False))
    for dy in (2, 1, 3):
        for d in range(2):
            x_msg(d, 0, dy, True).wait_recv()
        mm(piece(0, dy), False, (0, 1))
    for d in range(2):
        z_msg(d, 2, 1, True).wait_recv()
        x_msg(d, 1, 2, True).wait_recv()
    mm(piece(1, 2), False, (1,))
    early = rc(acc.at[pl.ds(2, 2)], R, ps.at[0], pr.at[0], twin)
    go(early)
    mm(piece(1, 2), False, (0,))
    for dy in (1, 3):
        for d in range(2):
            z_msg(d, dy, 1, True).wait_recv()
            x_msg(d, 1, dy, True).wait_recv()
    mm_last(1)
    late = rc(L, RL, ps.at[1], pr.at[1], twin)
    go(late)
    mm_last(0)
    for cp in others_in:
        cp.wait()
    early.wait_recv()
    late.wait_recv()

    for s in range(2):
        t = (acc[s, :, pl.ds(1024, 128)] + R[s, :, pl.ds(1024, 128)]
             + RL[s, :, pl.ds(1024, 128)].astype(F32)).astype(BF16)
        low[pl.ds(s * 256, 256), :] = t
        for i in range(2):
            pol[s, :, pl.ds(i * 512, 512)] = adapter_scale * jnp.dot(
                t[:, i * 64:(i + 1) * 64], up[i], preferred_element_type=F32)

    def token_weight(s, r):
        pos = r * 32 + lax.broadcasted_iota(jnp.int32, (32, 1), 0)
        sign = jnp.where(chosen[0] == s, 1.0, -1.0).astype(F32)
        return jnp.where(pos >= 256 - lengths[0, s], sign, 0.0)

    total = jnp.zeros((32, 512), F32)
    for s in range(2):
        def first_pass(r, total, s=s):
            rows = pl.ds(pl.multiple_of(r * 32, 32), 32)
            kr = acc[s, rows, pl.ds(0, 512)] + (
                R[s, rows, pl.ds(0, 512)] + RL[s, rows, pl.ds(0, 512)].astype(F32))
            vr = acc[s, rows, pl.ds(512, 512)] + (
                R[s, rows, pl.ds(512, 512)] + RL[s, rows, pl.ds(512, 512)].astype(F32))
            kp = kr + pol[s, rows, pl.ds(0, 512)]
            vp = vr + pol[s, rows, pl.ds(512, 512)]
            pol[s, rows, pl.ds(0, 512)] = kp
            pol[s, rows, pl.ds(512, 512)] = vp
            read = ro[s, rows, :].astype(F32)
            return total + token_weight(s, r) * (read * (kp * vp - kr * vr))
        total = lax.fori_loop(0, 8, first_pass, total)
    margin = jnp.sum(jnp.sum(total, axis=0, keepdims=True), axis=1, keepdims=True)
    pair_weight = -preference_beta * jax.nn.sigmoid(-preference_beta * margin)

    for s in range(2):
        def second_pass(r, carry, s=s):
            rows = pl.ds(pl.multiple_of(r * 32, 32), 32)
            whole = pl.ds(pl.multiple_of(s * 256 + r * 32, 32), 32)
            read = (pair_weight * token_weight(s, r)) * ro[s, rows, :].astype(F32)
            gk[whole, :] = (read * pol[s, rows, pl.ds(512, 512)]).astype(BF16)
            gv[whole, :] = (read * pol[s, rows, pl.ds(0, 512)]).astype(BF16)
            return carry
        lax.fori_loop(0, 8, second_pass, 0)

    nt = (((1,), (1,)), ((), ()))
    for i, g in enumerate((gk, gv)):
        BT[pl.ds(i * 64, 64), pl.ds(0, 512)] = (adapter_scale * lax.dot_general(
            up[i], g[...], nt, preferred_element_type=F32)).astype(BF16)
    b_cp = rc(BT.at[:, pl.ds(0, 512)], BT.at[:, pl.ds(512, 512)], ts.at[0], tr.at[0], twin)
    go(b_cp)
    low_t = jnp.transpose(low[...].astype(F32)).astype(BF16)
    for i, g in enumerate((gk, gv)):
        U[i] = adapter_scale * jnp.dot(
            low_t[i * 64:(i + 1) * 64, :], g[...], preferred_element_type=F32)
    u_cp = rc(U.at[1 - c], UT, ts.at[1], tr.at[1], twin)
    go(u_cp)
    b_cp.wait_recv()

    def grad(p):
        return jnp.dot(BT[...], H[p].reshape(1024, 512), preferred_element_type=F32)

    zd = []
    for dy in (2, 1, 3, 0):
        D[dy] = grad(piece(1, dy)).astype(BF16)
        for d in range(2):
            h = pl.ds(d * 64, 64)
            cp = rc(D.at[dy, h], RZ.at[dy, h], us.at[dy, d], ur.at[dy, d], z_to[d])
            go(cp)
            zd.append((dy, cp))

    u_cp.wait_recv()
    chip = U[c] + UT[...]
    for j in range(16):
        r, q = j // 4, j % 4
        US1[j] = chip[r * 16:(r + 1) * 16, q * 128:(q + 1) * 128].astype(BF16)

    def spread16(src, dst, send, recv):
        for k in (10, 9, 11, 8, 6, 14, 5, 13, 7, 15, 4, 12, 2, 1, 3):
            j = (me16 + k) % 16
            rc(src(j), dst.at[me16], send.at[k], recv.at[k], peer16(k)).start()

    def land16(src, dst, send, recv):
        def one(k, carry):
            j = (me16 + 16 - k) % 16
            rc(src(j), dst.at[j], send.at[k], recv.at[k], peer16(k)).wait_recv()
            return carry
        lax.fori_loop(1, 16, one, 0, unroll=True)

    def sent16(src, dst, send, recv):
        def one(k, carry):
            j = (me16 + k) % 16
            rc(src(j), dst.at[me16], send.at[k], recv.at[k], peer16(k)).wait_send()
            return carry
        lax.fori_loop(1, 16, one, 0, unroll=True)

    u_args = (lambda j: US1.at[j], US2, vs, vr)
    spread16(*u_args)
    US2[me16] = US1[me16]

    yd = []
    for dy in (2, 1, 3, 0):
        own = grad(piece(0, dy))
        for dd, cp in zd:
            if dd == dy:
                cp.wait_recv()
        t = own + RZ[dy].astype(F32)
        if dy:
            D2[dy] = t.astype(BF16)
            cp = rc(D2.at[dy], RY.at[dy], qs.at[dy], qr.at[dy], at_y(dy))
            go(cp)
            yd.append(cp)
        else:
            E[0] = t

    land16(*u_args)
    UA[...] = jnp.sum(US2[...].astype(F32), axis=0).astype(BF16)
    UB[fs] = UA[...]
    for k in range(1, 8):
        go(rc(UA, UB.at[fs], ws.at[k], wr.at[k], peer8(k)))

    for cp in yd:
        cp.wait_recv()
    t = E[0] + RY[1].astype(F32) + RY[2].astype(F32) + RY[3].astype(F32)
    S1[...] = jnp.transpose(t).astype(BF16).reshape(16, 32, 128)
    s_args = (lambda j: S1.at[j], S2, ss, sr)
    spread16(*s_args)
    S2[me16] = S1[me16]
    for k in range(1, 8):
        rc(UA, UB.at[(fs + 8 - k) % 8], ws.at[k], wr.at[k], peer8(k)).wait_recv()
    GU[c, me16] = jnp.sum(UB[...].astype(F32), axis=0).astype(BF16)
    gu_args = (lambda j: GU.at[c, me16], GU.at[c], es, er)
    spread16(*gu_args)
    land16(*s_args)
    GD[c, me16] = jnp.sum(S2[...].astype(F32), axis=0).astype(BF16)
    gd_args = (lambda j: GD.at[c, me16], GD.at[c], gs, gr)
    spread16(*gd_args)
    land16(*gu_args)
    go(rc(GU.at[c], GU.at[c], ts.at[3], tr.at[3], twin))
    land16(*gd_args)
    out = [rc(GU.at[c], GU.at[c], ts.at[3], tr.at[3], twin), rc(GD.at[c], GD.at[c], ts.at[2], tr.at[2], twin)]
    go(out[1])
    for cp in out:
        cp.wait_recv()
    for cp in started:
        cp.wait_send()
    for args in (u_args, s_args, gu_args, gd_args):
        sent16(*args)


def widen(gd, gu, od, ou):
    od[...] = gd[...].astype(F32).reshape(1024, 128)
    for core in range(2):
        for j in range(16):
            ou[core, pl.ds((j // 4) * 16, 16), pl.ds((j % 4) * 128, 128)] = gu[core, j].astype(F32)


def local(hidden, frozen_weight, adapter_down_weight, adapter_up_weight, readout, chosen, response_length):
    dma = pltpu.SemaphoreType.DMA
    vmem = pltpu.VMEM
    anywhere = pl.BlockSpec(memory_space=pl.ANY)
    smem = pl.BlockSpec(memory_space=pltpu.SMEM)
    gd, gu = pl.pallas_call(
        kernel,
        out_shape=(
            jax.ShapeDtypeStruct((2, 16, 32, 128), BF16),
            jax.ShapeDtypeStruct((2, 16, 16, 128), BF16),
        ),
        in_specs=[anywhere] * 5 + [smem] * 2,
        out_specs=(pl.BlockSpec(memory_space=pltpu.VMEM), pl.BlockSpec(memory_space=pltpu.VMEM)),
        scratch_shapes=[
            vmem((8, HALF, WIDE), BF16),
            vmem((8, 4, 256, HALF), BF16),
            vmem((4, 256, WIDE), F32),
            vmem((2, 256, WIDE), F32),
            vmem((2, 256, WIDE), BF16),
            vmem((2, 256, WIDE), BF16),
            vmem((2, 64, 512), BF16),
            vmem((2, 256, 512), BF16),
            vmem((2, 256, 1024), F32),
            vmem((512, 128), BF16),
            vmem((512, 512), BF16),
            vmem((512, 512), BF16),
            vmem((128, 1024), BF16),
            vmem((2, 64, 512), F32),
            vmem((64, 512), F32),
            vmem((16, 16, 128), BF16),
            vmem((16, 16, 128), BF16),
            vmem((16, 128), BF16),
            vmem((8, 16, 128), BF16),
            vmem((4, 128, 512), BF16),
            vmem((4, 128, 512), BF16),
            vmem((4, 128, 512), F32),
            vmem((4, 128, 512), BF16),
            vmem((4, 128, 512), BF16),
            vmem((16, 32, 128), BF16),
            vmem((16, 32, 128), BF16),
            dma((12,)),
            dma((8,)), dma((8,)),
            dma((2, 6)), dma((2, 6)),
            dma((2, 4, 2)), dma((2, 4, 2)),
            dma((2, 8)), dma((2, 8)),
            dma((2,)), dma((2,)),
            dma((4,)), dma((4,)),
            dma((4, 2)), dma((4, 2)),
            dma((16,)), dma((16,)),
            dma((4,)), dma((4,)),
            dma((8,)), dma((8,)),
            dma((16,)), dma((16,)),
            dma((16,)), dma((16,)),
            dma((16,)), dma((16,)),
            pltpu.SemaphoreType.REGULAR((6,)),
        ],
        compiler_params=pltpu.CompilerParams(
            collective_id=0, has_side_effects=True, vmem_limit_bytes=56 * 2**20
        ),
        cost_estimate=pl.CostEstimate(flops=12 * 10**9, bytes_accessed=12 * 10**6, transcendentals=1),
    )(hidden, frozen_weight, adapter_down_weight, adapter_up_weight, readout, chosen, response_length)
    return pl.pallas_call(
        widen,
        out_shape=(
            jax.ShapeDtypeStruct((1024, 128), F32),
            jax.ShapeDtypeStruct((2, 64, 512), F32),
        ),
        in_specs=[pl.BlockSpec(memory_space=pltpu.VMEM)] * 2,
        out_specs=(pl.BlockSpec(memory_space=pltpu.VMEM),) * 2,
        cost_estimate=pl.CostEstimate(flops=10**6, bytes_accessed=2 * 10**6, transcendentals=0),
    )(gd, gu)


def solution(mesh):
    placed = (
        P(("dp", "fsdp"), None, None, None),
        P("fsdp", None),
        P("fsdp", None),
        P(),
        P(("dp", "fsdp"), None, None, None),
        P(("dp", "fsdp")),
        P(("dp", "fsdp"), None),
    )
    return jax.shard_map(
        local, mesh=mesh, in_specs=placed, out_specs=(P("fsdp", None), P()), check_vma=False
    )
```
